256 devices in a mesh: dp: 32 (over z_lo, y, core), cout: 8 (over z_hi, x).
Axes of the slice: x: 4, y: 4, z: 8 (z_hi: 2, z_lo: 4; z = z_hi * 4 + z_lo), core: 2. Of those that a mesh axis runs over, the one named last changes fastest.
Arguments:
- images: bfloat16 [128, 512, 1024], P('dp', 'cout'), may hold values from -6 to 6
- styles: float32 [128, 512], P('dp'), may hold values from -5 to 5
- weight: bfloat16 [9, 512, 512], P(None, 'cout', 'dp'), may hold values from -0.09375 to 0.09375
- cotangent: bfloat16 [128, 512, 1024], P('dp', 'cout'), may hold values from -6 to 6
Outputs:
- output: bfloat16 [128, 512, 1024], P('dp', 'cout')
- input_grad: bfloat16 [128, 512, 1024], P('dp', 'cout')
- style_grad: float32 [128, 512], P('dp', 'cout')
- weight_grad: float32 [9, 512, 512], P(None, 'cout', 'dp')
The draws below stay inside these ranges and needn't reach their ends.
All inputs are finite; a program needn't handle non-finite values.
Results may differ from the reference program's by a relative error of at most 0.013.
Values may be sent and summed in bfloat16 or wider, within the bound.
No kernel may reach another device: no remote copies, remote signals or barrier semaphores. Data moves between devices by JAX's collectives and lax.ppermute only.
A program may use at most 192 MiB of HBM per device.

```python
import jax
import jax.numpy as jnp
from jax import lax

CIN = 512
COUT = 512
RES = 32
TAPS = 9
BATCH = 128
PIXELS = 1024
N_COUT = 8


def with_spikes(result, stream_key, source, target, shards_of, factor):
    owner, partner = [(jnp.arange(result.shape[dim]) // (result.shape[dim] // shards_of)).reshape([-1 if axis == dim else 1 for axis in range(result.ndim)]) for dim in (source, target)]
    chosen = jax.random.permutation(stream_key, shards_of)[partner]
    strong = (owner == chosen) | (owner == (partner + shards_of // 2) % shards_of)
    return jnp.where(strong, factor * result, result)


def levels(key, extent, split, smallest, largest):
    def one(axis_at, blocks):
        draws = jax.random.uniform(jax.random.fold_in(jax.random.fold_in(key, 6), axis_at), (blocks,), jnp.float32, smallest / len(split), largest / len(split))
        return jnp.repeat(jnp.exp(draws), extent[axis_at] // blocks).reshape((-1,) + (1,) * (len(extent) - axis_at - 1))

    factor_of = one(*split[0])
    for cut in split[1:]:
        factor_of = factor_of * one(*cut)
    return factor_of


def scatter_about(stream_key, extent, spread, limit, pieces=(), kind=jnp.bfloat16):
    gain = levels(stream_key, extent, pieces, -0.22, 0.18) if pieces else 1.0
    result = jax.random.normal(stream_key, extent, jnp.float32) * spread * gain
    return jnp.minimum(jnp.maximum(result, -limit), limit).astype(kind)


def gaussian_with(stream_key, dims, width, most, cuts, heavy, dtype=jnp.bfloat16):
    result = width * jax.random.normal(stream_key, dims, jnp.float32)
    if cuts:
        result = result * levels(stream_key, dims, cuts, -0.22, 0.18)
    return jnp.clip(with_spikes(result, jax.random.fold_in(stream_key, 3), *heavy), -most, most).astype(dtype)


def setup_inputs(seed: int = 0) -> dict:
    key_list = jax.random.split(jax.random.key(seed), 5)
    return {
        "images": gaussian_with(key_list[0], (BATCH, CIN, PIXELS), 1.0, 6.0, ((0, 32), (1, 8)), (0, 1, 32, 2.75)),
        "styles": scatter_about(key_list[1], (BATCH, CIN), 1.0, 5.0, ((0, 32),), jnp.float32),
        "weight": scatter_about(key_list[2], (TAPS, COUT, CIN), (CIN * TAPS) ** -0.5, 0.09375, ((1, 8), (2, 32))),
        "cotangent": scatter_about(key_list[3], (BATCH, COUT, PIXELS), 1.0, 6.0, ((0, 32), (1, 8))),
    }


epsilon = 1e-08
tap_steps = [(-1, -1), (-1, 0), (-1, 1), (0, -1), (0, 0), (0, 1), (1, -1), (1, 0), (1, 1)]

def displace(source, row_step, col_step, grid_side):
    length = source.shape[-1]
    margin = grid_side + 1
    offset = row_step * grid_side + col_step
    widths = [(0, 0)] * (source.ndim - 1) + [(margin, margin)]
    padded = jnp.pad(source, widths)
    moved = lax.slice_in_dim(padded, margin + offset, margin + offset + length, axis=source.ndim - 1)
    column = jnp.arange(length) % grid_side + col_step
    inside = (column >= 0) & (column < grid_side)
    return jnp.where(inside, moved, jnp.zeros_like(moved))

def round_trip(values):
    return lax.optimization_barrier(values.astype(jnp.bfloat16)).astype(jnp.float32)

def reference(images, styles, weight, cotangent):
    kernel_energy = lax.optimization_barrier(jnp.sum(jnp.square(weight.astype(jnp.float32)), axis=0))
    group = COUT // N_COUT
    length = RES * RES

    def step(carry, inputs):
        image, style, upstream = inputs
        modulated = (image.astype(jnp.float32) * style[:, None]).astype(jnp.bfloat16)
        energy = jnp.dot(kernel_energy, style * style, precision=lax.Precision.HIGHEST)
        demodulation = lax.rsqrt(energy + epsilon)
        convolved = jnp.zeros((COUT, length), jnp.float32)
        for tap_index, (row_step, col_step) in enumerate(tap_steps):
            product = jnp.dot(weight[tap_index], modulated, preferred_element_type=jnp.float32)
            convolved = convolved + displace(product, row_step, col_step, RES)
        output = (demodulation[:, None] * convolved).astype(jnp.bfloat16)
        grads = upstream.astype(jnp.float32)
        scaled = (grads * demodulation[:, None]).astype(jnp.bfloat16)
        norm_grad = lax.optimization_barrier(jnp.sum(grads * convolved, axis=1))
        energy_grad = -0.5 * norm_grad * demodulation ** 3
        moved = [displace(scaled, -row_step, -col_step, RES) for row_step, col_step in tap_steps]
        back_sum = jnp.zeros((CIN, length), jnp.float32)
        style_sum = jnp.zeros((CIN,), jnp.float32)
        for member in range(N_COUT):
            lower = member * group
            back_part = jnp.zeros((CIN, length), jnp.float32)
            for tap_index in range(TAPS):
                back_part = back_part + jnp.dot(weight[tap_index, lower:lower + group].T, moved[tap_index][lower:lower + group], preferred_element_type=jnp.float32)
            style_part = 2.0 * style * jnp.dot(energy_grad[lower:lower + group], kernel_energy[lower:lower + group], precision=lax.Precision.HIGHEST)
            back_sum = back_sum + round_trip(back_part)
            style_sum = style_sum + round_trip(style_part)
        input_grad = (back_sum * style[:, None]).astype(jnp.bfloat16)
        style_grad = lax.optimization_barrier(jnp.sum(back_sum * image.astype(jnp.float32), axis=1)) + style_sum
        weight_part = jnp.stack([jnp.dot(moved[tap_index], modulated.T, preferred_element_type=jnp.float32) for tap_index in range(TAPS)])
        radial = 2.0 * weight.astype(jnp.float32) * jnp.outer(energy_grad, style * style)[None]
        return (carry + weight_part + radial, (output, input_grad, style_grad))
    start = jnp.zeros((TAPS, COUT, CIN), jnp.float32)
    weight_total, (output, input_grad, style_grad) = lax.scan(step, start, (images, styles, cotangent))
    weight_grad = weight_total * (1.0 / BATCH)
    return (output, input_grad, style_grad, weight_grad)
```

```python
import jax
import jax.numpy as jnp
from jax import lax
from jax.experimental import pallas as pl
from jax.experimental.pallas import tpu as pltpu
from jax.sharding import PartitionSpec as P

RES = 32
epsilon = 1e-08
tap_steps = [(-1, -1), (-1, 0), (-1, 1), (0, -1), (0, 0), (0, 1), (1, -1), (1, 0), (1, 1)]
F32 = jnp.float32
BF16 = jnp.bfloat16
HIGH = lax.Precision.HIGHEST
BOTH = ("dp", "cout")
SIZES = {"l": 4, "y": 4, "c": 2, "h": 2, "x": 4}
MIB = 1 << 20


def flat_index(at):
    return ((at["l"] * 4 + at["y"]) * 2 + at["c"]) * 8 + at["h"] * 4 + at["x"]


def places(names):
    if not names:
        return [{}]
    return [{**rest, names[0]: v} for v in range(SIZES[names[0]]) for rest in places(names[1:])]


def exchange(blocks, along):
    others = [name for name in "lychx" if name not in along]
    groups = [[flat_index({**fixed, **at}) for at in places(along)] for fixed in places(others)]
    return lax.all_to_all(blocks, BOTH, 0, 0, axis_index_groups=groups, tiled=True)


def moved_by(value, name, step):
    pairs = []
    for at in places("lychx"):
        to = {**at, name: (at[name] + step) % SIZES[name]}
        pairs.append((flat_index(at), flat_index(to)))
    return lax.ppermute(value, BOTH, pairs)


def inside(row_step, col_step):
    pixel = lax.broadcasted_iota(jnp.int32, (1, RES * RES), 1)
    row = pixel // RES + row_step
    col = pixel % RES + col_step
    return (row >= 0) & (row < RES) & (col >= 0) & (col < RES)


def shifted(value, row_step, col_step):
    offset = row_step * RES + col_step
    if offset == 0:
        return value
    rolled = pltpu.roll(value, (-offset) % (RES * RES), 1)
    return jnp.where(inside(row_step, col_step), rolled, 0.0)


def back_body(place, style, cot, own, other, back, kernel_t, moved, energy_t, demod, scaled):
    y, core = place[0], place[1]

    @pl.loop(0, 16)
    def _(step):
        k, l = step // 4, step % 4
        for source, at_core in ((own, core), (other, 1 - core)):
            row = pl.multiple_of(((l * 4 + (y + k) % 4) * 2 + at_core) * 16, 16)
            piece = source[k, l]
            kernel_t[pl.ds(row, 16), :] = piece
            wide = piece.astype(F32)
            total = jnp.zeros((16, 256), F32)
            for t in range(9):
                part = wide[:, t * 256 : (t + 1) * 256]
                total = total + part * part
            energy_t[pl.ds(row, 16), :] = total

    row_style = style[...]
    energy = jnp.dot(row_style * row_style, energy_t[...], precision=HIGH, preferred_element_type=F32)
    demod_row = lax.rsqrt(energy + epsilon)
    demod[...] = jnp.transpose(jnp.broadcast_to(demod_row[:1], (128, 256)))
    for j in range(8):
        lanes = slice(j * 128, (j + 1) * 128)
        scaled[:, lanes] = (cot[:, lanes].astype(F32) * demod[...]).astype(BF16).astype(F32)

    @pl.loop(0, 8)
    def _(step):
        row = pl.multiple_of(step * 32, 32)
        value = scaled[pl.ds(row, 32), :]
        for t, (a, c) in enumerate(tap_steps):
            moved[pl.ds(t * 256 + row, 32), :] = shifted(value, -a, -c).astype(BF16)

    @pl.loop(0, 4)
    def _(step):
        lanes = pl.ds(pl.multiple_of(step * 256, 256), 256)
        back[:, lanes] = jnp.dot(
            kernel_t[...], moved[:, lanes], preferred_element_type=F32
        ).astype(BF16)


def main_body(
    place, style, cot, images, kernel_t, moved, energy_t, demod,
    out, send, keep, style_part, products, terms, radial, slope,
):
    y, core = place[0], place[1]

    @pl.loop(0, 4)
    def _(step):
        lanes = pl.ds(pl.multiple_of(step * 256, 256), 256)
        products[:, lanes] = lax.dot_general(
            kernel_t[...], images[:, lanes], (((0,), (0,)), ((), ())), preferred_element_type=F32
        )

    @pl.loop(0, 8)
    def _(step):
        row = pl.multiple_of(step * 32, 32)
        total = products[pl.ds(4 * 256 + row, 32), :]
        for t, (a, c) in enumerate(tap_steps):
            if t != 4:
                total = total + shifted(products[pl.ds(t * 256 + row, 32), :], a, c)
        factor = demod[pl.ds(row, 32), :]
        upstream = cot[pl.ds(row, 32), :].astype(F32)
        norm = jnp.sum(upstream * total, axis=1, keepdims=True)
        slope[pl.ds(row, 32), :] = -0.5 * norm * (factor * factor * factor)
        for j in range(8):
            lanes = slice(j * 128, (j + 1) * 128)
            out[pl.ds(row, 32), lanes] = (factor * total[:, lanes]).astype(BF16)

    slope_row = jnp.transpose(slope[...])
    row_style = style[...]
    style_part[...] = (2.0 * row_style) * lax.dot_general(
        slope_row[:8], energy_t[...], (((1,), (1,)), ((), ())),
        precision=HIGH, preferred_element_type=F32,
    )
    square = jnp.transpose(jnp.broadcast_to((row_style * row_style)[:1], (128, 512)))
    for j in range(2):
        lanes = slice(j * 128, (j + 1) * 128)
        radial[:, lanes] = 2.0 * square * slope_row[:1, lanes]

    @pl.loop(0, 9)
    def _(t):
        lanes = pl.ds(pl.multiple_of(t * 256, 256), 256)
        terms[...] = lax.dot_general(
            images[...], moved[lanes, :], (((1,), (1,)), ((), ())), preferred_element_type=F32
        ) + radial[...] * kernel_t[:, lanes].astype(F32)
        for k in range(4):
            for l in range(4):
                row = (l * 4 + (y + k) % 4) * 32
                mine = pl.multiple_of(row + core * 16, 16)
                theirs = pl.multiple_of(row + (1 - core) * 16, 16)
                keep[k, l, :, lanes] = terms[pl.ds(mine, 16), :]
                send[k, l, :, lanes] = terms[pl.ds(theirs, 16), :].astype(BF16)


def vmem(count):
    return [pl.BlockSpec(memory_space=pltpu.VMEM)] * count


def back_call(place, style, cot, own, other):
    shape = jax.ShapeDtypeStruct
    return pl.pallas_call(
        back_body,
        out_shape=(
            shape((512, 1024), BF16),
            shape((512, 2304), BF16),
            shape((2304, 1024), BF16),
            shape((512, 256), F32),
            shape((256, 128), F32),
        ),
        in_specs=[pl.BlockSpec(memory_space=pltpu.SMEM)] + vmem(4),
        out_specs=tuple(vmem(5)),
        scratch_shapes=[pltpu.VMEM((256, 1024), F32)],
        compiler_params=pltpu.CompilerParams(vmem_limit_bytes=28 * MIB),
        cost_estimate=pl.CostEstimate(
            flops=2 * 512 * 2304 * 1024, bytes_accessed=12 * MIB, transcendentals=256
        ),
        name="back",
    )(place, style, cot, own, other)


def main_call(place, style, cot, images, kernel_t, moved, energy_t, demod):
    shape = jax.ShapeDtypeStruct
    return pl.pallas_call(
        main_body,
        out_shape=(
            shape((256, 1024), BF16),
            shape((4, 4, 16, 2304), BF16),
            shape((4, 4, 16, 2304), F32),
            shape((8, 512), F32),
        ),
        in_specs=[pl.BlockSpec(memory_space=pltpu.SMEM)] + vmem(7),
        out_specs=tuple(vmem(4)),
        scratch_shapes=[
            pltpu.VMEM((2304, 1024), F32),
            pltpu.VMEM((512, 256), F32),
            pltpu.VMEM((512, 256), F32),
            pltpu.VMEM((256, 128), F32),
        ],
        compiler_params=pltpu.CompilerParams(vmem_limit_bytes=40 * MIB),
        cost_estimate=pl.CostEstimate(
            flops=4 * 512 * 2304 * 1024, bytes_accessed=16 * MIB, transcendentals=256
        ),
        name="main",
    )(place, style, cot, images, kernel_t, moved, energy_t, demod)


def on_device(images, styles, weight, cotangent):
    seat = lax.axis_index("cout")
    spot = lax.axis_index("dp")
    place = jnp.stack([(spot // 2) % 4, spot % 2]).astype(jnp.int32)
    local_styles = lax.dynamic_slice_in_dim(styles, seat * 64, 64, 1)
    style = jnp.broadcast_to(lax.dynamic_slice_in_dim(styles, seat % 4, 1, 0), (8, 512))

    packed = jnp.transpose(weight, (2, 0, 1)).reshape(16, 576)
    near = exchange(jnp.broadcast_to(packed[None], (16, 16, 576)), "lx")
    near = near.reshape(4, 4, 16, 9, 64).transpose(0, 2, 3, 1, 4).reshape(4, 16, 2304)
    own = jnp.stack([near] + [moved_by(near, "y", -k) for k in (1, 2, 3)])
    other = moved_by(own, "c", 1)

    cot = exchange(cotangent, "x").reshape(256, 1024)
    modulated = (images.astype(F32) * local_styles[:, :, None]).astype(BF16)
    whole = exchange(jnp.concatenate([modulated, modulated]), "hx").reshape(512, 1024)

    back, kernel_t, moved, energy_t, demod = back_call(place, style, cot, own, other)
    back_parts = exchange(back.reshape(8, 64, 1024), "hx").reshape(2, 4, 64, 1024)

    out, send, keep, style_part = main_call(
        place, style, cot, whole, kernel_t, moved, energy_t, demod
    )
    received = moved_by(send, "c", 1)
    output = exchange(out.reshape(4, 64, 1024), "x")
    style_parts = exchange(style_part[0].reshape(8, 1, 64), "hx").reshape(2, 4, 64)

    halves = (keep + received.astype(F32)).astype(BF16)
    quarters = halves[0].astype(F32)
    for k in (1, 2, 3):
        quarters = quarters + moved_by(halves[k], "y", k).astype(F32)
    blocks = quarters.astype(BF16).reshape(4, 16, 9, 4, 64).transpose(0, 3, 1, 2, 4)
    blocks = exchange(blocks.reshape(16, 16, 576), "lx")
    total = jnp.sum(blocks.astype(F32), axis=0) * (1.0 / 128)
    weight_grad = total.reshape(16, 9, 64).transpose(1, 2, 0)

    back_sum = back_parts[0].astype(F32) + back_parts[1].astype(F32)
    input_grad = (back_sum * local_styles[:, :, None]).astype(BF16)
    style_grad = jnp.sum(back_sum * images.astype(F32), axis=2) + style_parts[0] + style_parts[1]
    return (output, input_grad, style_grad, weight_grad)


def solution(mesh):
    return jax.shard_map(
        on_device,
        mesh=mesh,
        in_specs=(
            P("dp", "cout", None),
            P("dp", None),
            P(None, "cout", "dp"),
            P("dp", "cout", None),
        ),
        out_specs=(
            P("dp", "cout", None),
            P("dp", "cout", None),
            P("dp", "cout"),
            P(None, "cout", "dp"),
        ),
        check_vma=False,
    )
```

```python
import jax
import jax.numpy as jnp
from jax import lax
from jax.experimental import pallas as pl
from jax.experimental.pallas import tpu as pltpu
from jax.sharding import PartitionSpec as P

RES = 32
epsilon = 1e-08
tap_steps = [(-1, -1), (-1, 0), (-1, 1), (0, -1), (0, 0), (0, 1), (1, -1), (1, 0), (1, 1)]
F32 = jnp.float32
BF16 = jnp.bfloat16
HIGH = lax.Precision.HIGHEST
BOTH = ("dp", "cout")
SIZES = {"l": 4, "y": 4, "c": 2, "h": 2, "x": 4}
MIB = 1 << 20


def flat_index(at):
    return ((at["l"] * 4 + at["y"]) * 2 + at["c"]) * 8 + at["h"] * 4 + at["x"]


def places(names):
    if not names:
        return [{}]
    return [{**rest, names[0]: v} for v in range(SIZES[names[0]]) for rest in places(names[1:])]


def exchange(blocks, along):
    others = [name for name in "lychx" if name not in along]
    groups = [[flat_index({**fixed, **at}) for at in places(along)] for fixed in places(others)]
    return lax.all_to_all(blocks, BOTH, 0, 0, axis_index_groups=groups, tiled=True)


def moved_by(value, name, step):
    pairs = []
    for at in places("lychx"):
        to = {**at, name: (at[name] + step) % SIZES[name]}
        pairs.append((flat_index(at), flat_index(to)))
    return lax.ppermute(value, BOTH, pairs)


def inside(row_step, col_step):
    pixel = lax.broadcasted_iota(jnp.int32, (1, RES * RES), 1)
    row = pixel // RES + row_step
    col = pixel % RES + col_step
    return (row >= 0) & (row < RES) & (col >= 0) & (col < RES)


def shifted(value, row_step, col_step):
    offset = row_step * RES + col_step
    if offset == 0:
        return value
    rolled = pltpu.roll(value, (-offset) % (RES * RES), 1)
    return jnp.where(inside(row_step, col_step), rolled, 0.0)


def rows_of(place, k, l):
    return (((place[0] + l) % 4) * 4 + (place[1] + k) % 4) * 32


def image_grad_body(
    place, cot0, cot1, cot2, cot3, whole, moved_out, grad_out, moved, grad, images, sems
):
    bring = pltpu.make_async_copy(whole, images, sems.at[10])
    bring.start()
    for k, source in enumerate((cot0, cot1, cot2, cot3)):
        block = ((place[3] + 4 - k) % 4) * 64

        @pl.loop(0, 2)
        def _(half):
            value = source[pl.ds(pl.multiple_of(half * 32, 32), 32), :].astype(F32)
            for t, (a, c) in enumerate(tap_steps):
                row = pl.multiple_of(t * 256 + block + half * 32, 32)
                moved[pl.ds(row, 32), :] = shifted(value, -a, -c).astype(BF16)

    pltpu.make_async_copy(moved, moved_out, sems.at[9]).start()
    bring.wait()

    def leave(t):
        lanes = pl.ds(pl.multiple_of(t * 256, 256), 256)
        return pltpu.make_async_copy(grad.at[:, lanes], grad_out.at[:, lanes], sems.at[t])

    @pl.loop(0, 9)
    def _(t):
        lanes = pl.ds(pl.multiple_of(t * 256, 256), 256)
        grad[:, lanes] = lax.dot_general(
            images[...], moved[lanes, :], (((1,), (1,)), ((), ())), preferred_element_type=F32
        )
        leave(t).start()

    @pl.loop(0, 9)
    def _(t):
        leave(t).wait()

    pltpu.make_async_copy(moved, moved_out, sems.at[9]).wait()


def gradient_body(
    place, style, moved_in, grad_in, own0, own1, own2, own3, other0, other1, other2, other3,
    demod_out, send_out, keep_out, back_out, kernel_out,
    moved, grad, kernel_t, scaled_t, energy_t, inner, demod, send, keep, back, sems,
):
    core = place[2]
    sources = []
    for k, (own, other) in enumerate(
        ((own0, other0), (own1, other1), (own2, other2), (own3, other3))
    ):
        sources += [(k, own, core), (k, other, 1 - core)]

    def copy(index, source, target):
        return pltpu.make_async_copy(source, target, sems.at[index])

    copy(4, grad_in, grad).start()
    copy(5, moved_in, moved).start()
    for k, source, at_core in sources:

        @pl.loop(0, 4)
        def _(l):
            row = pl.multiple_of(rows_of(place, k, l) + at_core * 16, 16)
            piece = source[l]
            kernel_t[pl.ds(row, 16), :] = piece
            wide = piece.astype(F32)
            total = jnp.zeros((16, 256), F32)
            for t in range(9):
                part = wide[:, t * 256 : (t + 1) * 256]
                total = total + part * part
            energy_t[pl.ds(row, 16), :] = total

    row_style = style[...]
    square_row = row_style * row_style
    energy = jnp.dot(square_row, energy_t[...], precision=HIGH, preferred_element_type=F32)
    factor = lax.rsqrt(energy + epsilon)
    demod[...] = jnp.transpose(jnp.broadcast_to(factor[:1], (128, 256)))
    copy(0, demod, demod_out).start()
    copy(6, kernel_t, kernel_out).start()

    copy(4, grad_in, grad).wait()
    inner[...] = jnp.zeros((16, 256), F32)

    @pl.loop(0, 32)
    def _(step):
        row = pl.multiple_of(step * 16, 16)
        dots = jnp.zeros((16, 256), F32)
        for t in range(9):
            lanes = slice(t * 256, (t + 1) * 256)
            dots = dots + kernel_t[pl.ds(row, 16), lanes].astype(F32) * grad[pl.ds(row, 16), lanes]
        inner[...] += dots

    norm = jnp.sum(inner[...], axis=0, keepdims=True)
    slope = -0.5 * norm * (factor * factor * factor)
    style_col = jnp.transpose(jnp.broadcast_to(row_style[:1], (128, 512)))
    style_sum = jnp.sum(energy_t[...] * slope[:1], axis=1, keepdims=True)
    back[:, 1024:1152] = (2.0 * style_col * style_sum).astype(BF16)
    for j in range(2):
        lanes = slice(j * 128, (j + 1) * 128)
        energy_t[:, lanes] = 2.0 * (style_col * style_col) * slope[:1, lanes]

    @pl.loop(0, 16)
    def _(step):
        k, l = step // 4, step % 4
        for target, at_core in ((keep, core), (send, 1 - core)):
            row = pl.multiple_of(rows_of(place, k, l) + at_core * 16, 16)
            radial = energy_t[pl.ds(row, 16), :]
            for t in range(9):
                lanes = slice(t * 256, (t + 1) * 256)
                part = kernel_t[pl.ds(row, 16), lanes].astype(F32)
                term = grad[pl.ds(row, 16), lanes] * factor[:1] + part * radial
                target[k, l, :, lanes] = term.astype(target.dtype)
                scaled_t[pl.ds(row, 16), lanes] = (part * factor[:1]).astype(BF16)

    copy(1, send, send_out).start()
    copy(2, keep, keep_out).start()
    copy(5, moved_in, moved).wait()
    side = slice(1024, 1152)
    copy(3, back.at[:, side], back_out.at[:, side]).start()

    def back_copy(step):
        lanes = pl.ds(pl.multiple_of(step * 256, 256), 256)
        return copy(7 + step, back.at[:, lanes], back_out.at[:, lanes])

    @pl.loop(0, 4)
    def _(step):
        lanes = pl.ds(pl.multiple_of(step * 256, 256), 256)
        back[:, lanes] = jnp.dot(
            scaled_t[...], moved[:, lanes], preferred_element_type=F32
        ).astype(BF16)
        back_copy(step).start()

    copy(0, demod, demod_out).wait()
    copy(1, send, send_out).wait()
    copy(2, keep, keep_out).wait()
    copy(3, back.at[:, side], back_out.at[:, side]).wait()
    copy(6, kernel_t, kernel_out).wait()

    @pl.loop(0, 4)
    def _(step):
        back_copy(step).wait()


def forward_body(place, whole, kernel_in, demod_in, out, products, kernel_t, images, demod, sems):
    copies = [
        pltpu.make_async_copy(source, target, sems.at[index])
        for index, (source, target) in enumerate(
            ((kernel_in, kernel_t), (whole, images), (demod_in, demod))
        )
    ]
    for copy in copies:
        copy.start()
    for copy in copies:
        copy.wait()

    @pl.loop(0, 4)
    def _(step):
        lanes = pl.ds(pl.multiple_of(step * 256, 256), 256)
        products[:, lanes] = lax.dot_general(
            kernel_t[...], images[:, lanes], (((0,), (0,)), ((), ())), preferred_element_type=F32
        )

    @pl.loop(0, 8)
    def _(step):
        k, half = step // 2, step % 2
        row = pl.multiple_of(((place[3] + k) % 4) * 64 + half * 32, 32)
        total = products[pl.ds(4 * 256 + row, 32), :]
        for t, (a, c) in enumerate(tap_steps):
            if t != 4:
                total = total + shifted(products[pl.ds(t * 256 + row, 32), :], a, c)
        factor = demod[pl.ds(row, 32), :]
        for j in range(8):
            lanes = slice(j * 128, (j + 1) * 128)
            place_at = pl.ds(pl.multiple_of(half * 32, 32), 32)
            out[k, place_at, lanes] = (factor * total[:, lanes]).astype(BF16)


def pair_body(keep, received, *outs):
    for k, out in enumerate(outs):

        @pl.loop(0, 4)
        def _(l):
            out[l] = (keep[k, l] + received[k, l].astype(F32)).astype(BF16)


def quarter_body(place, part0, part1, part2, part3, out0, out1, out2, out3, sums):
    @pl.loop(0, 4)
    def _(l):
        total = part0[l].astype(F32)
        for part in (part1, part2, part3):
            total = total + part[l].astype(F32)
        sums[...] = total
        for k, out in enumerate((out0, out1, out2, out3)):
            pair = ((place[3] + k) % 4) // 2
            for t in range(9):
                start = pl.multiple_of(t * 256 + pair * 128, 128)
                out[l, t * 16 : (t + 1) * 16, :] = sums[:, pl.ds(start, 128)].astype(BF16)


def output_body(place, part0, part1, part2, part3, out, sems):
    copies = []
    for k, part in enumerate((part0, part1, part2, part3)):
        slot = (place[3] + 4 - k) % 4
        copies.append(pltpu.make_async_copy(part, out.at[slot], sems.at[k]))
    for copy in copies:
        copy.start()
    for copy in copies:
        copy.wait()


PRODUCT = 2 * 512 * 2304 * 1024
VM = pltpu.VMEM
HB = pltpu.HBM


def run(body, name, outs, out_space, scratch, mib, flops, *args, far=()):
    def space(index, arg):
        if arg.dtype == jnp.int32:
            return pltpu.SMEM
        return HB if index in far else VM

    return pl.pallas_call(
        body,
        out_shape=tuple(jax.ShapeDtypeStruct(*one) for one in outs),
        in_specs=[pl.BlockSpec(memory_space=space(*one)) for one in enumerate(args)],
        out_specs=tuple(pl.BlockSpec(memory_space=out_space) for _ in outs),
        scratch_shapes=scratch,
        compiler_params=pltpu.CompilerParams(vmem_limit_bytes=mib * MIB),
        cost_estimate=pl.CostEstimate(flops=flops, bytes_accessed=MIB, transcendentals=256),
        name=name,
    )(*args)


def ring_take(parts, start):
    return lax.dynamic_slice_in_dim(jnp.concatenate([parts, parts]), start, 4, 0)


def on_device(images, styles, weight, cotangent):
    seat = lax.axis_index("cout")
    spot = lax.axis_index("dp")
    column = seat % 4
    place = jnp.stack([spot // 8, (spot // 2) % 4, spot % 2, column]).astype(jnp.int32)
    local_styles = lax.dynamic_slice_in_dim(styles, seat * 64, 64, 1)
    style = jnp.broadcast_to(lax.dynamic_slice_in_dim(styles, column, 1, 0), (8, 512))

    packed = jnp.transpose(weight, (2, 0, 1)).reshape(9, 1024)
    stages = [packed] + [moved_by(packed, "l", -k) for k in (1, 2, 3)]
    rows = jnp.pad(jnp.concatenate(stages), ((0, 4), (0, 0)))
    modulated = (images.astype(F32) * local_styles[:, :, None]).astype(BF16)
    rows, twice = lax.optimization_barrier((rows, jnp.concatenate([modulated, modulated])))
    whole = exchange(twice, "hx").reshape(512, 1024)

    turned = [lax.dynamic_index_in_dim(cotangent, (column + k) % 4, 0, False) for k in range(4)]
    cots = [turned[0]] + [
        moved_by(jnp.concatenate([turned[k], rows]), "x", k) for k in (1, 2, 3)
    ]
    taps = jnp.stack([rows[:36]] + [cots[k][64:100] for k in (3, 2, 1)])
    taps = ring_take(taps, (4 - column) % 4)
    near = taps.reshape(4, 4, 16, 9, 64).transpose(1, 2, 3, 0, 4).reshape(4, 16, 2304)
    own = [near] + [moved_by(near, "y", -k) for k in (1, 2, 3)]
    kernels = own + [moved_by(one, "c", 1) for one in own]

    moved, grad = run(
        image_grad_body,
        "image_grad",
        [((2304, 1024), BF16), ((512, 2304), F32)],
        HB,
        [
            VM((2304, 1024), BF16),
            VM((512, 2304), F32),
            VM((512, 1024), BF16),
            pltpu.SemaphoreType.DMA((11,)),
        ],
        16,
        12 * PRODUCT,
        place,
        *cots,
        whole,
        far=(5,),
    )
    blocks = (4, 4, 16, 2304)
    demod, send, keep, back, kernel_t = run(
        gradient_body,
        "gradient",
        [
            ((256, 128), F32),
            (blocks, BF16),
            (blocks, F32),
            ((512, 1152), BF16),
            ((512, 2304), BF16),
        ],
        HB,
        [
            VM((2304, 1024), BF16),
            VM((512, 2304), F32),
            VM((512, 2304), BF16),
            VM((512, 2304), BF16),
            VM((512, 256), F32),
            VM((16, 256), F32),
            VM((256, 128), F32),
            VM(blocks, BF16),
            VM(blocks, F32),
            VM((512, 1152), BF16),
            pltpu.SemaphoreType.DMA((11,)),
        ],
        30,
        2 * PRODUCT,
        place,
        style,
        moved,
        grad,
        *kernels,
        far=(2, 3),
    )
    received = moved_by(send, "c", 1)
    (out,) = run(
        forward_body,
        "forward",
        [((4, 64, 1024), BF16)],
        VM,
        [
            VM((2304, 1024), F32),
            VM((512, 2304), BF16),
            VM((512, 1024), BF16),
            VM((256, 128), F32),
            pltpu.SemaphoreType.DMA((3,)),
        ],
        18,
        PRODUCT,
        place,
        whole,
        kernel_t,
        demod,
        far=(1, 2, 3),
    )
    outs = [out[0]] + [moved_by(out[k], "x", k) for k in (1, 2, 3)]
    (output,) = run(
        output_body, "output", [((4, 64, 1024), BF16)], HB, [pltpu.SemaphoreType.DMA((4,))],
        4, 10**6, place, *outs,
    )

    halves = run(
        pair_body, "pair_sum", [((4, 16, 2304), BF16)] * 4, VM, [], 8, 10**7, keep, received
    )
    halves, back = lax.optimization_barrier((halves, back))
    back_parts = exchange(back.reshape(8, 64, 1152), "hx").reshape(2, 4, 64, 1152)
    quarters = [halves[0]] + [moved_by(halves[k], "y", k) for k in (1, 2, 3)]
    pieces = run(
        quarter_body, "quarter_sum", [((4, 144, 128), BF16)] * 4, VM, [VM((16, 2304), F32)],
        6, 10**7, place, *quarters,
    )
    total = pieces[0].astype(F32)
    for k in (1, 2, 3):
        total = total + moved_by(pieces[k], "x", k).astype(F32)
    pieces = total.astype(BF16)
    total = pieces[0].astype(F32)
    for k in (1, 2, 3):
        total = total + moved_by(pieces[k], "l", k).astype(F32)
    total = lax.dynamic_slice_in_dim(total * (1.0 / 128), (column % 2) * 64, 64, 1)
    weight_grad = total.reshape(9, 16, 64).transpose(0, 2, 1)

    back_sum = back_parts[0].astype(F32) + back_parts[1].astype(F32)
    input_grad = (back_sum[:, :, :1024] * local_styles[:, :, None]).astype(BF16)
    style_grad = jnp.sum(back_sum[:, :, :1024] * images.astype(F32), axis=2) + back_sum[:, :, 1024]
    return (output, input_grad, style_grad, weight_grad)


def solution(mesh):
    return jax.shard_map(
        on_device,
        mesh=mesh,
        in_specs=(
            P("dp", "cout", None),
            P("dp", None),
            P(None, "cout", "dp"),
            P("dp", "cout", None),
        ),
        out_specs=(
            P("dp", "cout", None),
            P("dp", "cout", None),
            P("dp", "cout"),
            P(None, "cout", "dp"),
        ),
        check_vma=False,
    )
```

```python
import jax
import jax.numpy as jnp
from jax import lax
from jax.experimental import pallas as pl
from jax.experimental.pallas import tpu as pltpu
from jax.sharding import PartitionSpec as P

RES = 32
epsilon = 1e-08
tap_steps = [(-1, -1), (-1, 0), (-1, 1), (0, -1), (0, 0), (0, 1), (1, -1), (1, 0), (1, 1)]
F32 = jnp.float32
BF16 = jnp.bfloat16
HIGH = lax.Precision.HIGHEST
BOTH = ("dp", "cout")
SIZES = {"l": 4, "y": 4, "c": 2, "h": 2, "x": 4}
MIB = 1 << 20


def flat_index(at):
    return ((at["l"] * 4 + at["y"]) * 2 + at["c"]) * 8 + at["h"] * 4 + at["x"]


def places(names):
    if not names:
        return [{}]
    return [{**rest, names[0]: v} for v in range(SIZES[names[0]]) for rest in places(names[1:])]


def exchange(blocks, along):
    others = [name for name in "lychx" if name not in along]
    groups = [[flat_index({**fixed, **at}) for at in places(along)] for fixed in places(others)]
    return lax.all_to_all(blocks, BOTH, 0, 0, axis_index_groups=groups, tiled=True)


def moved_by(value, name, step):
    pairs = []
    for at in places("lychx"):
        to = {**at, name: (at[name] + step) % SIZES[name]}
        pairs.append((flat_index(at), flat_index(to)))
    return lax.ppermute(value, BOTH, pairs)


def inside(row_step, col_step):
    pixel = lax.broadcasted_iota(jnp.int32, (1, RES * RES), 1)
    row = pixel // RES + row_step
    col = pixel % RES + col_step
    return (row >= 0) & (row < RES) & (col >= 0) & (col < RES)


def shifted(value, row_step, col_step):
    offset = row_step * RES + col_step
    if offset == 0:
        return value
    rolled = pltpu.roll(value, (-offset) % (RES * RES), 1)
    return jnp.where(inside(row_step, col_step), rolled, 0.0)


def rows_of(place, k, l):
    return (((place[0] + l) % 4) * 4 + (place[1] + k) % 4) * 32


def ready_body(place, whole, out):
    del whole
    for index in range(4):
        out[index] = place[index]


def gradient_body(
    place, style, cot0, cot1, cot2, cot3, whole, own0, own1, own2, own3, other0, other1, other2, other3,
    demod_out, send_out, keep_out, back_out, kernel_out,
    moved, grad, images, kernel_t, scaled_t, energy_t, inner, demod, send, keep, back, sems,
):
    core = place[2]
    sources = []
    for k, (own, other) in enumerate(
        ((own0, other0), (own1, other1), (own2, other2), (own3, other3))
    ):
        sources += [(k, own, core), (k, other, 1 - core)]

    def copy(index, source, target):
        return pltpu.make_async_copy(source, target, sems.at[index])

    copy(4, whole, images).start()
    for k, source in enumerate((cot0, cot1, cot2, cot3)):
        block = ((place[3] + 4 - k) % 4) * 64

        @pl.loop(0, 2)
        def _(half):
            value = source[pl.ds(pl.multiple_of(half * 32, 32), 32), :].astype(F32)
            for t, (a, c) in enumerate(tap_steps):
                row = pl.multiple_of(t * 256 + block + half * 32, 32)
                moved[pl.ds(row, 32), :] = shifted(value, -a, -c).astype(BF16)

    for k, source, at_core in sources:

        @pl.loop(0, 4)
        def _(l):
            row = pl.multiple_of(rows_of(place, k, l) + at_core * 16, 16)
            piece = source[l]
            kernel_t[pl.ds(row, 16), :] = piece
            wide = piece.astype(F32)
            total = jnp.zeros((16, 256), F32)
            for t in range(9):
                part = wide[:, t * 256 : (t + 1) * 256]
                total = total + part * part
            energy_t[pl.ds(row, 16), :] = total

    row_style = style[...]
    style_col = jnp.transpose(jnp.broadcast_to(row_style[:1], (128, 512)))
    square = style_col * style_col
    energy = jnp.concatenate(
        [
            jnp.sum(energy_t[:, j * 128 : (j + 1) * 128] * square, axis=0, keepdims=True)
            for j in range(2)
        ],
        axis=1,
    )
    factor = lax.rsqrt(energy + epsilon)
    demod[...] = jnp.transpose(jnp.broadcast_to(factor, (128, 256)))
    copy(0, demod, demod_out).start()
    copy(6, kernel_t, kernel_out).start()

    copy(4, whole, images).wait()

    @pl.loop(0, 9)
    def _(t):
        lanes = pl.ds(pl.multiple_of(t * 256, 256), 256)
        grad[:, lanes] = lax.dot_general(
            images[...], moved[lanes, :], (((1,), (1,)), ((), ())), preferred_element_type=F32
        )

    inner[...] = jnp.zeros((16, 256), F32)

    @pl.loop(0, 32)
    def _(step):
        row = pl.multiple_of(step * 16, 16)
        dots = jnp.zeros((16, 256), F32)
        for t in range(9):
            lanes = slice(t * 256, (t + 1) * 256)
            part = kernel_t[pl.ds(row, 16), lanes].astype(F32)
            dots = dots + part * grad[pl.ds(row, 16), lanes]
            scaled_t[pl.ds(row, 16), lanes] = (part * factor).astype(BF16)
        inner[...] += dots

    norm = jnp.sum(inner[...], axis=0, keepdims=True)
    slope = -0.5 * norm * (factor * factor * factor)
    style_sum = jnp.sum(energy_t[...] * slope[:1], axis=1, keepdims=True)
    back[:, 1024:1152] = (2.0 * style_col * style_sum).astype(BF16)
    for j in range(2):
        lanes = slice(j * 128, (j + 1) * 128)
        energy_t[:, lanes] = 2.0 * square * slope[:1, lanes]

    side = slice(1024, 1152)
    copy(3, back.at[:, side], back_out.at[:, side]).start()

    def back_copy(step):
        lanes = pl.ds(pl.multiple_of(step * 256, 256), 256)
        return copy(7 + step, back.at[:, lanes], back_out.at[:, lanes])

    def terms_copy(step):
        return copy(11 + step, send.at[step], send_out.at[step])

    def keep_copy(step):
        return copy(15 + step, keep.at[step], keep_out.at[step])

    @pl.loop(0, 4)
    def _(step):
        lanes = pl.ds(pl.multiple_of(step * 256, 256), 256)
        back[:, lanes] = jnp.dot(
            scaled_t[...], moved[:, lanes], preferred_element_type=F32
        ).astype(BF16)
        for l in range(4):
            for target, at_core in ((keep, core), (send, 1 - core)):
                row = pl.multiple_of(rows_of(place, step, l) + at_core * 16, 16)
                radial = energy_t[pl.ds(row, 16), :]
                for t in range(9):
                    taps = slice(t * 256, (t + 1) * 256)
                    part = kernel_t[pl.ds(row, 16), taps].astype(F32)
                    term = grad[pl.ds(row, 16), taps] * factor + part * radial
                    target[step, l, :, taps] = term.astype(target.dtype)
        back_copy(step).start()
        terms_copy(step).start()
        keep_copy(step).start()

    copy(0, demod, demod_out).wait()
    copy(3, back.at[:, side], back_out.at[:, side]).wait()
    copy(6, kernel_t, kernel_out).wait()

    @pl.loop(0, 4)
    def _(step):
        back_copy(step).wait()
        terms_copy(step).wait()
        keep_copy(step).wait()


def forward_body(place, whole, kernel_in, demod_in, out, products, kernel_t, images, demod, sems):
    copies = [
        pltpu.make_async_copy(source, target, sems.at[index])
        for index, (source, target) in enumerate(
            ((kernel_in, kernel_t), (whole, images), (demod_in, demod))
        )
    ]
    for copy in copies:
        copy.start()
    for copy in copies:
        copy.wait()

    @pl.loop(0, 4)
    def _(step):
        lanes = pl.ds(pl.multiple_of(step * 256, 256), 256)
        products[:, lanes] = lax.dot_general(
            kernel_t[...], images[:, lanes], (((0,), (0,)), ((), ())), preferred_element_type=F32
        )

    @pl.loop(0, 8)
    def _(step):
        k, half = step // 2, step % 2
        row = pl.multiple_of(((place[3] + k) % 4) * 64 + half * 32, 32)
        total = products[pl.ds(4 * 256 + row, 32), :]
        for t, (a, c) in enumerate(tap_steps):
            if t != 4:
                total = total + shifted(products[pl.ds(t * 256 + row, 32), :], a, c)
        factor = demod[pl.ds(row, 32), :]
        for j in range(8):
            lanes = slice(j * 128, (j + 1) * 128)
            place_at = pl.ds(pl.multiple_of(half * 32, 32), 32)
            out[k, place_at, lanes] = (factor * total[:, lanes]).astype(BF16)


def pair_body(keep, received, *outs):
    for k, out in enumerate(outs):

        @pl.loop(0, 4)
        def _(l):
            out[l] = (keep[k, l] + received[k, l].astype(F32)).astype(BF16)


def quarter_body(place, part0, part1, part2, part3, out0, out1, out2, out3, sums):
    low = lax.broadcasted_iota(jnp.int32, (16, 128), 1) < 64

    @pl.loop(0, 4)
    def _(l):
        total = part0[l].astype(F32)
        for part in (part1, part2, part3):
            total = total + part[l].astype(F32)
        sums[...] = total
        for k, out in enumerate((out0, out1, out2, out3)):
            column = (place[3] + k) % 4
            even = column % 2 == 0

            def block(t):
                start = pl.multiple_of(t * 256 + (column // 2) * 128, 128)
                value = sums[:, pl.ds(start, 128)]
                return value, pltpu.roll(value, 64, 1)

            for pair in range(5):
                first, first_rolled = block(2 * pair)
                left = jnp.where(even, first, first_rolled)
                right = jnp.zeros((16, 128), F32)
                if pair < 4:
                    second, second_rolled = block(2 * pair + 1)
                    right = jnp.where(even, second_rolled, second)
                packed = jnp.where(low, left, right).astype(BF16)
                out[l, pair * 16 : (pair + 1) * 16, :] = packed


def output_body(place, part0, part1, part2, part3, out, sems):
    copies = []
    for k, part in enumerate((part0, part1, part2, part3)):
        slot = (place[3] + 4 - k) % 4
        copies.append(pltpu.make_async_copy(part, out.at[slot], sems.at[k]))
    for copy in copies:
        copy.start()
    for copy in copies:
        copy.wait()


PRODUCT = 2 * 512 * 2304 * 1024
VM = pltpu.VMEM
HB = pltpu.HBM


def run(body, name, outs, out_space, scratch, mib, flops, *args, far=()):
    def space(index, arg):
        if arg.dtype == jnp.int32:
            return pltpu.SMEM
        return HB if index in far else VM

    return pl.pallas_call(
        body,
        out_shape=tuple(jax.ShapeDtypeStruct(*one) for one in outs),
        in_specs=[pl.BlockSpec(memory_space=space(*one)) for one in enumerate(args)],
        out_specs=tuple(pl.BlockSpec(memory_space=out_space) for _ in outs),
        scratch_shapes=scratch,
        compiler_params=pltpu.CompilerParams(vmem_limit_bytes=mib * MIB),
        cost_estimate=pl.CostEstimate(flops=flops, bytes_accessed=MIB, transcendentals=256),
        name=name,
    )(*args)


def ring_take(parts, start):
    return lax.dynamic_slice_in_dim(jnp.concatenate([parts, parts]), start, 4, 0)


def on_device(images, styles, weight, cotangent):
    seat = lax.axis_index("cout")
    spot = lax.axis_index("dp")
    column = seat % 4
    place = jnp.stack([spot // 8, (spot // 2) % 4, spot % 2, column]).astype(jnp.int32)
    local_styles = lax.dynamic_slice_in_dim(styles, seat * 64, 64, 1)
    style = jnp.broadcast_to(lax.dynamic_slice_in_dim(styles, column, 1, 0), (8, 512))

    packed = jnp.transpose(weight, (2, 0, 1)).reshape(9, 1024)
    stages = [packed] + [moved_by(packed, "l", -k) for k in (1, 2, 3)]
    rows = jnp.pad(jnp.concatenate(stages), ((0, 4), (0, 0)))
    modulated = (images.astype(F32) * local_styles[:, :, None]).astype(BF16)
    rows, twice = lax.optimization_barrier((rows, jnp.concatenate([modulated, modulated])))
    whole = exchange(twice, "hx").reshape(512, 1024)

    sides = [rows] + [moved_by(rows, "x", k) for k in (1, 2, 3)]
    taps = jnp.stack([sides[k][:36] for k in (0, 3, 2, 1)])
    taps = ring_take(taps, (4 - column) % 4)
    near = taps.reshape(4, 4, 16, 9, 64).transpose(1, 2, 3, 0, 4).reshape(4, 16, 2304)
    turned = [lax.dynamic_index_in_dim(cotangent, (column + k) % 4, 0, False) for k in range(4)]
    near, *turned = lax.optimization_barrier((near, *turned))
    cots = [turned[0]] + [moved_by(turned[k], "x", k) for k in (1, 2, 3)]
    own = [near] + [moved_by(near, "y", -k) for k in (1, 2, 3)]
    kernels = own + [moved_by(one, "c", 1) for one in own]

    (ready,) = run(
        ready_body, "ready", [((4,), jnp.int32)], pltpu.SMEM, [], 1, 12 * PRODUCT, place, whole,
        far=(1,),
    )
    blocks = (4, 4, 16, 2304)
    demod, send, keep, back, kernel_t = run(
        gradient_body,
        "gradient",
        [
            ((256, 128), F32),
            (blocks, BF16),
            (blocks, F32),
            ((512, 1152), BF16),
            ((512, 2304), BF16),
        ],
        HB,
        [
            VM((2304, 1024), BF16),
            VM((512, 2304), F32),
            VM((512, 1024), BF16),
            VM((512, 2304), BF16),
            VM((512, 2304), BF16),
            VM((512, 256), F32),
            VM((16, 256), F32),
            VM((256, 128), F32),
            VM(blocks, BF16),
            VM(blocks, F32),
            VM((512, 1152), BF16),
            pltpu.SemaphoreType.DMA((19,)),
        ],
        32,
        2 * PRODUCT,
        ready,
        style,
        *cots,
        whole,
        *kernels,
        far=(6,),
    )
    received = moved_by(send, "c", 1)
    (out,) = run(
        forward_body,
        "forward",
        [((4, 64, 1024), BF16)],
        VM,
        [
            VM((2304, 1024), F32),
            VM((512, 2304), BF16),
            VM((512, 1024), BF16),
            VM((256, 128), F32),
            pltpu.SemaphoreType.DMA((3,)),
        ],
        18,
        20 * PRODUCT,
        place,
        whole,
        kernel_t,
        demod,
        far=(1, 2, 3),
    )
    halves = run(
        pair_body, "pair_sum", [((4, 16, 2304), BF16)] * 4, VM, [], 8, 10**7, keep, received
    )
    halves, back = lax.optimization_barrier((halves, back))
    back_parts = exchange(back.reshape(8, 64, 1152), "hx").reshape(2, 4, 64, 1152)
    quarters = [halves[0]] + [moved_by(halves[k], "y", k) for k in (1, 2, 3)]
    pieces = run(
        quarter_body, "quarter_sum", [((4, 80, 128), BF16)] * 4, VM, [VM((16, 2304), F32)],
        6, 10**7, place, *quarters,
    )
    total = pieces[0].astype(F32)
    for k in (1, 2, 3):
        total = total + moved_by(pieces[k], "x", k).astype(F32)
    pieces = total.astype(BF16)
    pieces, out = lax.optimization_barrier((pieces, out))
    outs = [out[0]] + [moved_by(out[k], "x", k) for k in (1, 2, 3)]
    (output,) = run(
        output_body, "output", [((4, 64, 1024), BF16)], HB, [pltpu.SemaphoreType.DMA((4,))],
        4, 10**6, place, *outs,
    )

    parts = [pieces[0]] + [moved_by(pieces[k], "l", k) for k in (1, 2, 3)]
    back_sum = back_parts[0].astype(F32) + back_parts[1].astype(F32)
    input_grad = (back_sum[:, :, :1024] * local_styles[:, :, None]).astype(BF16)
    style_grad = jnp.sum(back_sum[:, :, :1024] * images.astype(F32), axis=2) + back_sum[:, :, 1024]
    input_grad, style_grad, *parts = lax.optimization_barrier((input_grad, style_grad, *parts))
    total = sum((part.astype(F32) for part in parts[1:]), parts[0].astype(F32))
    total = (total * (1.0 / 128)).reshape(5, 16, 2, 64)
    weight_grad = total.transpose(0, 2, 3, 1).reshape(10, 64, 16)[:9]
    return (output, input_grad, style_grad, weight_grad)


def solution(mesh):
    return jax.shard_map(
        on_device,
        mesh=mesh,
        in_specs=(
            P("dp", "cout", None),
            P("dp", None),
            P(None, "cout", "dp"),
            P("dp", "cout", None),
        ),
        out_specs=(
            P("dp", "cout", None),
            P("dp", "cout", None),
            P("dp", "cout"),
            P(None, "cout", "dp"),
        ),
        check_vma=False,
    )
```

```python
import jax
import jax.numpy as jnp
from jax import lax
from jax.experimental import pallas as pl
from jax.experimental.pallas import tpu as pltpu
from jax.sharding import PartitionSpec as P

RES = 32
epsilon = 1e-08
tap_steps = [(-1, -1), (-1, 0), (-1, 1), (0, -1), (0, 0), (0, 1), (1, -1), (1, 0), (1, 1)]
F32 = jnp.float32
BF16 = jnp.bfloat16
HIGH = lax.Precision.HIGHEST
BOTH = ("dp", "cout")
SIZES = {"l": 4, "y": 4, "c": 2, "h": 2, "x": 4}
MIB = 1 << 20


def flat_index(at):
    return ((at["l"] * 4 + at["y"]) * 2 + at["c"]) * 8 + at["h"] * 4 + at["x"]


def places(names):
    if not names:
        return [{}]
    return [{**rest, names[0]: v} for v in range(SIZES[names[0]]) for rest in places(names[1:])]


def exchange(blocks, along):
    others = [name for name in "lychx" if name not in along]
    groups = [[flat_index({**fixed, **at}) for at in places(along)] for fixed in places(others)]
    return lax.all_to_all(blocks, BOTH, 0, 0, axis_index_groups=groups, tiled=True)


def moved_by(value, name, step):
    pairs = []
    for at in places("lychx"):
        to = {**at, name: (at[name] + step) % SIZES[name]}
        pairs.append((flat_index(at), flat_index(to)))
    return lax.ppermute(value, BOTH, pairs)


def inside(row_step, col_step):
    pixel = lax.broadcasted_iota(jnp.int32, (1, RES * RES), 1)
    row = pixel // RES + row_step
    col = pixel % RES + col_step
    return (row >= 0) & (row < RES) & (col >= 0) & (col < RES)


def shifted(value, row_step, col_step):
    offset = row_step * RES + col_step
    if offset == 0:
        return value
    rolled = pltpu.roll(value, (-offset) % (RES * RES), 1)
    return jnp.where(inside(row_step, col_step), rolled, 0.0)


def rows_of(place, k, l):
    return (((place[0] + l) % 4) * 4 + (place[1] + k) % 4) * 32


def ready_body(place, whole, out):
    del whole
    for index in range(4):
        out[index] = place[index]


def gradient_body(
    place, style, cot0, cot1, cot2, cot3, whole, own0, own1, own2, own3, other0, other1, other2, other3,
    demod_out, send_out, keep_out, back_out, kernel_out,
    moved, grad, images, kernel_t, scaled_t, energy_t, inner, demod, send, keep, back, sems,
):
    core = place[2]
    sources = []
    for k, (own, other) in enumerate(
        ((own0, other0), (own1, other1), (own2, other2), (own3, other3))
    ):
        sources += [(k, own, core), (k, other, 1 - core)]

    def copy(index, source, target):
        return pltpu.make_async_copy(source, target, sems.at[index])

    copy(4, whole, images).start()
    for k, source in enumerate((cot0, cot1, cot2, cot3)):
        block = ((place[3] + 4 - k) % 4) * 64

        @pl.loop(0, 2)
        def _(half):
            value = source[pl.ds(pl.multiple_of(half * 32, 32), 32), :].astype(F32)
            for t, (a, c) in enumerate(tap_steps):
                row = pl.multiple_of(t * 256 + block + half * 32, 32)
                moved[pl.ds(row, 32), :] = shifted(value, -a, -c).astype(BF16)

    for k, source, at_core in sources:

        @pl.loop(0, 4)
        def _(l):
            row = pl.multiple_of(rows_of(place, k, l) + at_core * 16, 16)
            piece = source[l]
            kernel_t[pl.ds(row, 16), :] = piece
            wide = piece.astype(F32)
            total = jnp.zeros((16, 256), F32)
            for t in range(9):
                part = wide[:, t * 256 : (t + 1) * 256]
                total = total + part * part
            energy_t[pl.ds(row, 16), :] = total

    row_style = style[...]
    style_col = jnp.transpose(jnp.broadcast_to(row_style[:1], (128, 512)))
    square = style_col * style_col
    energy = jnp.concatenate(
        [
            jnp.sum(energy_t[:, j * 128 : (j + 1) * 128] * square, axis=0, keepdims=True)
            for j in range(2)
        ],
        axis=1,
    )
    factor = lax.rsqrt(energy + epsilon)
    demod[...] = jnp.transpose(jnp.broadcast_to(factor, (128, 256)))
    copy(0, demod, demod_out).start()
    copy(6, kernel_t, kernel_out).start()

    copy(4, whole, images).wait()

    @pl.loop(0, 9)
    def _(t):
        lanes = pl.ds(pl.multiple_of(t * 256, 256), 256)
        grad[:, lanes] = lax.dot_general(
            images[...], moved[lanes, :], (((1,), (1,)), ((), ())), preferred_element_type=F32
        )

    inner[...] = jnp.zeros((16, 256), F32)

    @pl.loop(0, 32)
    def _(step):
        row = pl.multiple_of(step * 16, 16)
        dots = jnp.zeros((16, 256), F32)
        for t in range(9):
            lanes = slice(t * 256, (t + 1) * 256)
            part = kernel_t[pl.ds(row, 16), lanes].astype(F32)
            dots = dots + part * grad[pl.ds(row, 16), lanes]
            scaled_t[pl.ds(row, 16), lanes] = (part * factor).astype(BF16)
        inner[...] += dots

    norm = jnp.sum(inner[...], axis=0, keepdims=True)
    slope = -0.5 * norm * (factor * factor * factor)
    style_sum = jnp.sum(energy_t[...] * slope[:1], axis=1, keepdims=True)
    back[:, 1024:1152] = (2.0 * style_col * style_sum).astype(BF16)
    for j in range(2):
        lanes = slice(j * 128, (j + 1) * 128)
        energy_t[:, lanes] = 2.0 * square * slope[:1, lanes]

    side = slice(1024, 1152)
    copy(3, back.at[:, side], back_out.at[:, side]).start()

    def back_copy(step):
        lanes = pl.ds(pl.multiple_of(step * 256, 256), 256)
        return copy(7 + step, back.at[:, lanes], back_out.at[:, lanes])

    def terms_copy(step):
        return copy(11 + step, send.at[step], send_out.at[step])

    def keep_copy(step):
        return copy(15 + step, keep.at[step], keep_out.at[step])

    @pl.loop(0, 4)
    def _(step):
        lanes = pl.ds(pl.multiple_of(step * 256, 256), 256)
        back[:, lanes] = jnp.dot(
            scaled_t[...], moved[:, lanes], preferred_element_type=F32
        ).astype(BF16)
        for l in range(4):
            for target, at_core in ((keep, core), (send, 1 - core)):
                row = pl.multiple_of(rows_of(place, step, l) + at_core * 16, 16)
                radial = energy_t[pl.ds(row, 16), :]
                for t in range(9):
                    taps = slice(t * 256, (t + 1) * 256)
                    part = kernel_t[pl.ds(row, 16), taps].astype(F32)
                    term = grad[pl.ds(row, 16), taps] * factor + part * radial
                    target[step, l, :, taps] = term.astype(target.dtype)
        back_copy(step).start()
        terms_copy(step).start()
        keep_copy(step).start()

    copy(0, demod, demod_out).wait()
    copy(3, back.at[:, side], back_out.at[:, side]).wait()
    copy(6, kernel_t, kernel_out).wait()

    @pl.loop(0, 4)
    def _(step):
        back_copy(step).wait()
        terms_copy(step).wait()
        keep_copy(step).wait()


def forward_body(place, whole, kernel_in, demod_in, out, products, kernel_t, images, demod, sems):
    copies = [
        pltpu.make_async_copy(source, target, sems.at[index])
        for index, (source, target) in enumerate(
            ((kernel_in, kernel_t), (whole, images), (demod_in, demod))
        )
    ]
    for copy in copies:
        copy.start()
    for copy in copies:
        copy.wait()

    @pl.loop(0, 4)
    def _(step):
        lanes = pl.ds(pl.multiple_of(step * 256, 256), 256)
        products[:, lanes] = lax.dot_general(
            kernel_t[...], images[:, lanes], (((0,), (0,)), ((), ())), preferred_element_type=F32
        )

    @pl.loop(0, 8)
    def _(step):
        k, half = step // 2, step % 2
        row = pl.multiple_of(((place[3] + k) % 4) * 64 + half * 32, 32)
        total = products[pl.ds(4 * 256 + row, 32), :]
        for t, (a, c) in enumerate(tap_steps):
            if t != 4:
                total = total + shifted(products[pl.ds(t * 256 + row, 32), :], a, c)
        factor = demod[pl.ds(row, 32), :]
        for j in range(8):
            lanes = slice(j * 128, (j + 1) * 128)
            place_at = pl.ds(pl.multiple_of(half * 32, 32), 32)
            out[k, place_at, lanes] = (factor * total[:, lanes]).astype(BF16)


def pair_body(keep, received, *outs):
    for k, out in enumerate(outs):

        @pl.loop(0, 4)
        def _(l):
            out[l] = (keep[k, l] + received[k, l].astype(F32)).astype(BF16)


def quarter_body(place, part0, part1, part2, part3, out0, out1, out2, out3, sums):
    low = lax.broadcasted_iota(jnp.int32, (16, 128), 1) < 64

    @pl.loop(0, 4)
    def _(l):
        total = part0[l].astype(F32)
        for part in (part1, part2, part3):
            total = total + part[l].astype(F32)
        sums[...] = total
        for k, out in enumerate((out0, out1, out2, out3)):
            column = (place[3] + k) % 4
            even = column % 2 == 0

            def block(t):
                start = pl.multiple_of(t * 256 + (column // 2) * 128, 128)
                value = sums[:, pl.ds(start, 128)]
                return value, pltpu.roll(value, 64, 1)

            for pair in range(5):
                first, first_rolled = block(2 * pair)
                left = jnp.where(even, first, first_rolled)
                right = jnp.zeros((16, 128), F32)
                if pair < 4:
                    second, second_rolled = block(2 * pair + 1)
                    right = jnp.where(even, second_rolled, second)
                packed = jnp.where(low, left, right).astype(BF16)
                out[l, pair * 16 : (pair + 1) * 16, :] = packed


def finish_body(
    place, part0, part1, part2, part3, back, images, scale, out, input_grad, style_grad, sems
):
    copies = []
    for k, part in enumerate((part0, part1, part2, part3)):
        slot = (place[3] + 4 - k) % 4
        copies.append(pltpu.make_async_copy(part, out.at[slot], sems.at[k]))
    for copy in copies:
        copy.start()
    lane = lax.broadcasted_iota(jnp.int32, (64, 128), 1)
    columns = jnp.zeros((64, 128), F32)
    for b in range(4):
        total = jnp.zeros((64, 128), F32)
        for j in range(8):
            lanes = slice(j * 128, (j + 1) * 128)
            value = back[0, b, :, lanes].astype(F32) + back[1, b, :, lanes].astype(F32)
            input_grad[b, :, lanes] = (value * scale[b]).astype(BF16)
            total = total + value * images[b, :, lanes].astype(F32)
        side = slice(1024, 1152)
        side = back[0, b, :, side].astype(F32) + back[1, b, :, side].astype(F32)
        column = jnp.sum(total, axis=1, keepdims=True) + side[:, :1]
        columns = jnp.where(lane == b, column, columns)
    style_grad[...] = jnp.transpose(columns)[:4]
    for copy in copies:
        copy.wait()


PRODUCT = 2 * 512 * 2304 * 1024
VM = pltpu.VMEM
HB = pltpu.HBM


def run(body, name, outs, out_space, scratch, mib, flops, *args, far=()):
    def space(index, arg):
        if arg.dtype == jnp.int32:
            return pltpu.SMEM
        return HB if index in far else VM

    return pl.pallas_call(
        body,
        out_shape=tuple(jax.ShapeDtypeStruct(*one) for one in outs),
        in_specs=[pl.BlockSpec(memory_space=space(*one)) for one in enumerate(args)],
        out_specs=tuple(
            pl.BlockSpec(memory_space=out_space[n] if isinstance(out_space, tuple) else out_space)
            for n in range(len(outs))
        ),
        scratch_shapes=scratch,
        compiler_params=pltpu.CompilerParams(vmem_limit_bytes=mib * MIB),
        cost_estimate=pl.CostEstimate(flops=flops, bytes_accessed=MIB, transcendentals=256),
        name=name,
    )(*args)


def ring_take(parts, start):
    return lax.dynamic_slice_in_dim(jnp.concatenate([parts, parts]), start, 4, 0)


def on_device(images, styles, weight, cotangent):
    seat = lax.axis_index("cout")
    spot = lax.axis_index("dp")
    column = seat % 4
    place = jnp.stack([spot // 8, (spot // 2) % 4, spot % 2, column]).astype(jnp.int32)
    local_styles = lax.dynamic_slice_in_dim(styles, seat * 64, 64, 1)
    style = jnp.broadcast_to(lax.dynamic_slice_in_dim(styles, column, 1, 0), (8, 512))

    packed = jnp.transpose(weight, (2, 0, 1)).reshape(9, 1024)
    stages = [packed] + [moved_by(packed, "l", -k) for k in (1, 2, 3)]
    rows = jnp.pad(jnp.concatenate(stages), ((0, 4), (0, 0)))
    scale = jnp.broadcast_to(local_styles[:, :, None], (4, 64, 128))
    modulated = (images.astype(F32) * local_styles[:, :, None]).astype(BF16)
    rows, twice = lax.optimization_barrier((rows, jnp.concatenate([modulated, modulated])))
    whole = exchange(twice, "hx").reshape(512, 1024)

    sides = [rows] + [moved_by(rows, "x", k) for k in (1, 2, 3)]
    taps = jnp.stack([sides[k][:36] for k in (0, 3, 2, 1)])
    taps = ring_take(taps, (4 - column) % 4)
    near = taps.reshape(4, 4, 16, 9, 64).transpose(1, 2, 3, 0, 4).reshape(4, 16, 2304)
    turned = [lax.dynamic_index_in_dim(cotangent, (column + k) % 4, 0, False) for k in range(4)]
    near, *turned = lax.optimization_barrier((near, *turned))
    cots = [turned[0]] + [moved_by(turned[k], "x", k) for k in (1, 2, 3)]
    own = [near] + [moved_by(near, "y", -k) for k in (1, 2, 3)]
    kernels = own + [moved_by(one, "c", 1) for one in own]

    (ready,) = run(
        ready_body, "ready", [((4,), jnp.int32)], pltpu.SMEM, [], 1, 12 * PRODUCT, place, whole,
        far=(1,),
    )
    blocks = (4, 4, 16, 2304)
    demod, send, keep, back, kernel_t = run(
        gradient_body,
        "gradient",
        [
            ((256, 128), F32),
            (blocks, BF16),
            (blocks, F32),
            ((512, 1152), BF16),
            ((512, 2304), BF16),
        ],
        HB,
        [
            VM((2304, 1024), BF16),
            VM((512, 2304), F32),
            VM((512, 1024), BF16),
            VM((512, 2304), BF16),
            VM((512, 2304), BF16),
            VM((512, 256), F32),
            VM((16, 256), F32),
            VM((256, 128), F32),
            VM(blocks, BF16),
            VM(blocks, F32),
            VM((512, 1152), BF16),
            pltpu.SemaphoreType.DMA((19,)),
        ],
        32,
        2 * PRODUCT,
        ready,
        style,
        *cots,
        whole,
        *kernels,
        far=(6,),
    )
    received = moved_by(send, "c", 1)
    (out,) = run(
        forward_body,
        "forward",
        [((4, 64, 1024), BF16)],
        VM,
        [
            VM((2304, 1024), F32),
            VM((512, 2304), BF16),
            VM((512, 1024), BF16),
            VM((256, 128), F32),
            pltpu.SemaphoreType.DMA((3,)),
        ],
        18,
        20 * PRODUCT,
        place,
        whole,
        kernel_t,
        demod,
        far=(1, 2, 3),
    )
    halves = run(
        pair_body, "pair_sum", [((4, 16, 2304), BF16)] * 4, VM, [], 8, 10**7, keep, received
    )
    halves, back = lax.optimization_barrier((halves, back))
    back_parts = exchange(back.reshape(8, 64, 1152), "hx").reshape(2, 4, 64, 1152)
    quarters = [halves[0]] + [moved_by(halves[k], "y", k) for k in (1, 2, 3)]
    pieces = run(
        quarter_body, "quarter_sum", [((4, 80, 128), BF16)] * 4, VM, [VM((16, 2304), F32)],
        6, 10**7, place, *quarters,
    )
    total = pieces[0].astype(F32)
    for k in (1, 2, 3):
        total = total + moved_by(pieces[k], "x", k).astype(F32)
    pieces = total.astype(BF16)
    pieces, out = lax.optimization_barrier((pieces, out))
    outs = [out[0]] + [moved_by(out[k], "x", k) for k in (1, 2, 3)]
    parts = [pieces[0]] + [moved_by(pieces[k], "l", k) for k in (1, 2, 3)]
    output, input_grad, style_grad = run(
        finish_body,
        "finish",
        [((4, 64, 1024), BF16), ((4, 64, 1024), BF16), ((4, 64), F32)],
        (HB, VM, VM),
        [pltpu.SemaphoreType.DMA((4,))],
        8,
        10**7,
        place,
        *outs,
        back_parts,
        images,
        scale,
    )
    input_grad, style_grad, *parts = lax.optimization_barrier((input_grad, style_grad, *parts))
    total = sum((part.astype(F32) for part in parts[1:]), parts[0].astype(F32))
    total = (total * (1.0 / 128)).reshape(5, 16, 2, 64)
    weight_grad = total.transpose(0, 2, 3, 1).reshape(10, 64, 16)[:9]
    return (output, input_grad, style_grad, weight_grad)


def solution(mesh):
    return jax.shard_map(
        on_device,
        mesh=mesh,
        in_specs=(
            P("dp", "cout", None),
            P("dp", None),
            P(None, "cout", "dp"),
            P("dp", "cout", None),
        ),
        out_specs=(
            P("dp", "cout", None),
            P("dp", "cout", None),
            P("dp", "cout"),
            P(None, "cout", "dp"),
        ),
        check_vma=False,
    )
```

```python
import jax
import jax.numpy as jnp
from jax import lax
from jax.experimental import pallas as pl
from jax.experimental.pallas import tpu as pltpu
from jax.sharding import PartitionSpec as P

RES = 32
epsilon = 1e-08
tap_steps = [(-1, -1), (-1, 0), (-1, 1), (0, -1), (0, 0), (0, 1), (1, -1), (1, 0), (1, 1)]
F32 = jnp.float32
BF16 = jnp.bfloat16
HIGH = lax.Precision.HIGHEST
BOTH = ("dp", "cout")
SIZES = {"l": 4, "y": 4, "c": 2, "h": 2, "x": 4}
MIB = 1 << 20


def flat_index(at):
    return ((at["l"] * 4 + at["y"]) * 2 + at["c"]) * 8 + at["h"] * 4 + at["x"]


def places(names):
    if not names:
        return [{}]
    return [{**rest, names[0]: v} for v in range(SIZES[names[0]]) for rest in places(names[1:])]


def exchange(blocks, along):
    others = [name for name in "lychx" if name not in along]
    groups = [[flat_index({**fixed, **at}) for at in places(along)] for fixed in places(others)]
    return lax.all_to_all(blocks, BOTH, 0, 0, axis_index_groups=groups, tiled=True)


def moved_by(value, name, step):
    pairs = []
    for at in places("lychx"):
        to = {**at, name: (at[name] + step) % SIZES[name]}
        pairs.append((flat_index(at), flat_index(to)))
    return lax.ppermute(value, BOTH, pairs)


def inside(row_step, col_step):
    pixel = lax.broadcasted_iota(jnp.int32, (1, RES * RES), 1)
    row = pixel // RES + row_step
    col = pixel % RES + col_step
    return (row >= 0) & (row < RES) & (col >= 0) & (col < RES)


def shifted(value, row_step, col_step):
    offset = row_step * RES + col_step
    if offset == 0:
        return value
    rolled = pltpu.roll(value, (-offset) % (RES * RES), 1)
    return jnp.where(inside(row_step, col_step), rolled, 0.0)


def rows_of(place, k, l):
    return (((place[0] + l) % 4) * 4 + (place[1] + k) % 4) * 32


def ready_body(style, whole, out):
    del whole
    out[...] = style[...]


def gradient_body(
    place, style, cot0, cot1, cot2, cot3, whole, own0, own1, own2, own3, other0, other1, other2, other3,
    demod_out, send_out, keep_out, back_out, kernel_out,
    moved, grad, images, kernel_t, scaled_t, energy_t, inner, demod, send, keep, back, sems,
):
    core = place[2]
    sources = []
    for k, (own, other) in enumerate(
        ((own0, other0), (own1, other1), (own2, other2), (own3, other3))
    ):
        sources += [(k, own, core), (k, other, 1 - core)]

    def copy(index, source, target):
        return pltpu.make_async_copy(source, target, sems.at[index])

    copy(4, whole, images).start()
    for k, source in enumerate((cot0, cot1, cot2, cot3)):
        block = ((place[3] + 4 - k) % 4) * 64

        @pl.loop(0, 2)
        def _(half):
            value = source[pl.ds(pl.multiple_of(half * 32, 32), 32), :].astype(F32)
            for t, (a, c) in enumerate(tap_steps):
                row = pl.multiple_of(t * 256 + block + half * 32, 32)
                moved[pl.ds(row, 32), :] = shifted(value, -a, -c).astype(BF16)

    for k, source, at_core in sources:

        @pl.loop(0, 4)
        def _(l):
            row = pl.multiple_of(rows_of(place, k, l) + at_core * 16, 16)
            piece = source[l]
            kernel_t[pl.ds(row, 16), :] = piece
            wide = piece.astype(F32)
            total = jnp.zeros((16, 256), F32)
            for t in range(9):
                part = wide[:, t * 256 : (t + 1) * 256]
                total = total + part * part
            energy_t[pl.ds(row, 16), :] = total

    row_style = style[...]
    style_col = jnp.transpose(jnp.broadcast_to(row_style[:1], (128, 512)))
    square = style_col * style_col
    energy = jnp.concatenate(
        [
            jnp.sum(energy_t[:, j * 128 : (j + 1) * 128] * square, axis=0, keepdims=True)
            for j in range(2)
        ],
        axis=1,
    )
    factor = lax.rsqrt(energy + epsilon)
    demod[...] = jnp.transpose(jnp.broadcast_to(factor, (128, 256)))
    copy(0, demod, demod_out).start()
    copy(6, kernel_t, kernel_out).start()

    copy(4, whole, images).wait()

    @pl.loop(0, 9)
    def _(t):
        lanes = pl.ds(pl.multiple_of(t * 256, 256), 256)
        grad[:, lanes] = lax.dot_general(
            images[...], moved[lanes, :], (((1,), (1,)), ((), ())), preferred_element_type=F32
        )

    inner[...] = jnp.zeros((16, 256), F32)

    @pl.loop(0, 32)
    def _(step):
        row = pl.multiple_of(step * 16, 16)
        dots = jnp.zeros((16, 256), F32)
        for t in range(9):
            lanes = slice(t * 256, (t + 1) * 256)
            part = kernel_t[pl.ds(row, 16), lanes].astype(F32)
            dots = dots + part * grad[pl.ds(row, 16), lanes]
            scaled_t[pl.ds(row, 16), lanes] = (part * factor).astype(BF16)
        inner[...] += dots

    norm = jnp.sum(inner[...], axis=0, keepdims=True)
    slope = -0.5 * norm * (factor * factor * factor)
    style_sum = jnp.sum(energy_t[...] * slope[:1], axis=1, keepdims=True)
    back[:, 1024:1152] = (2.0 * style_col * style_sum).astype(BF16)
    for j in range(2):
        lanes = slice(j * 128, (j + 1) * 128)
        energy_t[:, lanes] = 2.0 * square * slope[:1, lanes]

    side = slice(1024, 1152)
    copy(3, back.at[:, side], back_out.at[:, side]).start()

    def back_copy(step):
        lanes = pl.ds(pl.multiple_of(step * 256, 256), 256)
        return copy(7 + step, back.at[:, lanes], back_out.at[:, lanes])

    def terms_copy(step):
        return copy(11 + step, send.at[step], send_out.at[step])

    def keep_copy(step):
        return copy(15 + step, keep.at[step], keep_out.at[step])

    @pl.loop(0, 4)
    def _(step):
        lanes = pl.ds(pl.multiple_of(step * 256, 256), 256)
        back[:, lanes] = jnp.dot(
            scaled_t[...], moved[:, lanes], preferred_element_type=F32
        ).astype(BF16)
        for l in range(4):
            for target, at_core in ((keep, core), (send, 1 - core)):
                row = pl.multiple_of(rows_of(place, step, l) + at_core * 16, 16)
                radial = energy_t[pl.ds(row, 16), :]
                for t in range(9):
                    taps = slice(t * 256, (t + 1) * 256)
                    part = kernel_t[pl.ds(row, 16), taps].astype(F32)
                    term = grad[pl.ds(row, 16), taps] * factor + part * radial
                    target[step, l, :, taps] = term.astype(target.dtype)
        back_copy(step).start()
        terms_copy(step).start()
        keep_copy(step).start()

    copy(0, demod, demod_out).wait()
    copy(3, back.at[:, side], back_out.at[:, side]).wait()
    copy(6, kernel_t, kernel_out).wait()

    @pl.loop(0, 4)
    def _(step):
        back_copy(step).wait()
        terms_copy(step).wait()
        keep_copy(step).wait()


def flip_body(kernel_in, out, kernel_t, sems):
    def enter(t):
        lanes = pl.ds(pl.multiple_of(t * 256, 256), 256)
        return pltpu.make_async_copy(kernel_in.at[:, lanes], kernel_t.at[:, lanes], sems.at[t])

    @pl.loop(0, 9)
    def _(t):
        enter(t).start()

    @pl.loop(0, 9)
    def _(t):
        enter(t).wait()
        part = pl.ds(pl.multiple_of(t * 256, 256), 256)
        out[part, :] = jnp.transpose(kernel_t[:, part])


def forward_body(place, whole, kernel, demod_in, out, products, images, demod, sems):
    copies = [
        pltpu.make_async_copy(source, target, sems.at[index])
        for index, (source, target) in enumerate(((whole, images), (demod_in, demod)))
    ]
    for copy in copies:
        copy.start()
    for copy in copies:
        copy.wait()

    @pl.loop(0, 4)
    def _(step):
        lanes = pl.ds(pl.multiple_of(step * 256, 256), 256)
        products[:, lanes] = jnp.dot(
            kernel[...], images[:, lanes], preferred_element_type=F32
        )

    @pl.loop(0, 8)
    def _(step):
        k, half = step // 2, step % 2
        row = pl.multiple_of(((place[3] + k) % 4) * 64 + half * 32, 32)
        total = products[pl.ds(4 * 256 + row, 32), :]
        for t, (a, c) in enumerate(tap_steps):
            if t != 4:
                total = total + shifted(products[pl.ds(t * 256 + row, 32), :], a, c)
        factor = demod[pl.ds(row, 32), :]
        for j in range(8):
            lanes = slice(j * 128, (j + 1) * 128)
            place_at = pl.ds(pl.multiple_of(half * 32, 32), 32)
            out[k, place_at, lanes] = (factor * total[:, lanes]).astype(BF16)


def pair_body(keep, received, *outs):
    for k, out in enumerate(outs):

        @pl.loop(0, 4)
        def _(l):
            out[l] = (keep[k, l] + received[k, l].astype(F32)).astype(BF16)


def quarter_body(place, part0, part1, part2, part3, out0, out1, out2, out3, sums):
    low = lax.broadcasted_iota(jnp.int32, (16, 128), 1) < 64

    @pl.loop(0, 4)
    def _(l):
        total = part0[l].astype(F32)
        for part in (part1, part2, part3):
            total = total + part[l].astype(F32)
        sums[...] = total
        for k, out in enumerate((out0, out1, out2, out3)):
            column = (place[3] + k) % 4
            even = column % 2 == 0

            def block(t):
                start = pl.multiple_of(t * 256 + (column // 2) * 128, 128)
                value = sums[:, pl.ds(start, 128)]
                return value, pltpu.roll(value, 64, 1)

            for pair in range(5):
                first, first_rolled = block(2 * pair)
                left = jnp.where(even, first, first_rolled)
                right = jnp.zeros((16, 128), F32)
                if pair < 4:
                    second, second_rolled = block(2 * pair + 1)
                    right = jnp.where(even, second_rolled, second)
                packed = jnp.where(low, left, right).astype(BF16)
                out[l, pair * 16 : (pair + 1) * 16, :] = packed


def finish_body(
    place, part0, part1, part2, part3, back, images, scale, out, input_grad, style_grad, sems
):
    copies = []
    for k, part in enumerate((part0, part1, part2, part3)):
        slot = (place[3] + 4 - k) % 4
        copies.append(pltpu.make_async_copy(part, out.at[slot], sems.at[k]))
    for copy in copies:
        copy.start()
    lane = lax.broadcasted_iota(jnp.int32, (64, 128), 1)
    columns = jnp.zeros((64, 128), F32)
    for b in range(4):
        total = jnp.zeros((64, 128), F32)
        for j in range(8):
            lanes = slice(j * 128, (j + 1) * 128)
            value = back[0, b, :, lanes].astype(F32) + back[1, b, :, lanes].astype(F32)
            input_grad[b, :, lanes] = (value * scale[b]).astype(BF16)
            total = total + value * images[b, :, lanes].astype(F32)
        side = slice(1024, 1152)
        side = back[0, b, :, side].astype(F32) + back[1, b, :, side].astype(F32)
        column = jnp.sum(total, axis=1, keepdims=True) + side[:, :1]
        columns = jnp.where(lane == b, column, columns)
    style_grad[...] = jnp.transpose(columns)[:4]
    for copy in copies:
        copy.wait()


PRODUCT = 2 * 512 * 2304 * 1024
VM = pltpu.VMEM
HB = pltpu.HBM


def run(body, name, outs, out_space, scratch, mib, flops, *args, far=()):
    def space(index, arg):
        if arg.dtype == jnp.int32:
            return pltpu.SMEM
        return HB if index in far else VM

    return pl.pallas_call(
        body,
        out_shape=tuple(jax.ShapeDtypeStruct(*one) for one in outs),
        in_specs=[pl.BlockSpec(memory_space=space(*one)) for one in enumerate(args)],
        out_specs=tuple(
            pl.BlockSpec(memory_space=out_space[n] if isinstance(out_space, tuple) else out_space)
            for n in range(len(outs))
        ),
        scratch_shapes=scratch,
        compiler_params=pltpu.CompilerParams(vmem_limit_bytes=mib * MIB),
        cost_estimate=pl.CostEstimate(flops=flops, bytes_accessed=MIB, transcendentals=256),
        name=name,
    )(*args)


def ring_take(parts, start):
    return lax.dynamic_slice_in_dim(jnp.concatenate([parts, parts]), start, 4, 0)


def on_device(images, styles, weight, cotangent):
    seat = lax.axis_index("cout")
    spot = lax.axis_index("dp")
    column = seat % 4
    place = jnp.stack([spot // 8, (spot // 2) % 4, spot % 2, column]).astype(jnp.int32)
    local_styles = lax.dynamic_slice_in_dim(styles, seat * 64, 64, 1)
    style = jnp.broadcast_to(lax.dynamic_slice_in_dim(styles, column, 1, 0), (8, 512))

    packed = jnp.transpose(weight, (2, 0, 1)).reshape(9, 1024)
    stages = [packed] + [moved_by(packed, "l", -k) for k in (1, 2, 3)]
    rows = jnp.pad(jnp.concatenate(stages), ((0, 4), (0, 0)))
    scale = jnp.broadcast_to(local_styles[:, :, None], (4, 64, 128))
    modulated = (images.astype(F32) * local_styles[:, :, None]).astype(BF16)
    rows, twice = lax.optimization_barrier((rows, jnp.concatenate([modulated, modulated])))
    whole = exchange(twice, "hx").reshape(512, 1024)

    sides = [rows] + [moved_by(rows, "x", k) for k in (1, 2, 3)]
    taps = jnp.stack([sides[k][:36] for k in (0, 3, 2, 1)])
    taps = ring_take(taps, (4 - column) % 4)
    near = taps.reshape(4, 4, 16, 9, 64).transpose(1, 2, 3, 0, 4).reshape(4, 16, 2304)
    turned = [lax.dynamic_index_in_dim(cotangent, (column + k) % 4, 0, False) for k in range(4)]
    near, *turned = lax.optimization_barrier((near, *turned))
    cots = [turned[0]] + [moved_by(turned[k], "x", k) for k in (1, 2, 3)]
    own = [near] + [moved_by(near, "y", -k) for k in (1, 2, 3)]
    kernels = own + [moved_by(one, "c", 1) for one in own]

    (ready,) = run(
        ready_body, "ready", [((8, 512), F32)], VM, [], 1, 12 * PRODUCT, style, whole,
        far=(1,),
    )
    blocks = (4, 4, 16, 2304)
    demod, send, keep, back, kernel_t = run(
        gradient_body,
        "gradient",
        [
            ((256, 128), F32),
            (blocks, BF16),
            (blocks, F32),
            ((512, 1152), BF16),
            ((512, 2304), BF16),
        ],
        HB,
        [
            VM((2304, 1024), BF16),
            VM((512, 2304), F32),
            VM((512, 1024), BF16),
            VM((512, 2304), BF16),
            VM((512, 2304), BF16),
            VM((512, 256), F32),
            VM((16, 256), F32),
            VM((256, 128), F32),
            VM(blocks, BF16),
            VM(blocks, F32),
            VM((512, 1152), BF16),
            pltpu.SemaphoreType.DMA((19,)),
        ],
        32,
        2 * PRODUCT,
        place,
        ready,
        *cots,
        whole,
        *kernels,
        far=(6,),
    )
    received = moved_by(send, "c", 1)
    halves = run(
        pair_body, "pair_sum", [((4, 16, 2304), BF16)] * 4, VM, [], 8, 10**7, keep, received
    )
    halves, back = lax.optimization_barrier((halves, back))
    back_parts = exchange(back.reshape(8, 64, 1152), "hx").reshape(2, 4, 64, 1152)
    quarters = [halves[0]] + [moved_by(halves[k], "y", k) for k in (1, 2, 3)]
    (kernel,) = run(
        flip_body, "flip", [((2304, 512), BF16)], VM,
        [VM((512, 2304), BF16), pltpu.SemaphoreType.DMA((9,))], 8, 10**7, kernel_t, far=(0,),
    )
    kernel, *quarters = lax.optimization_barrier((kernel, *quarters))
    (out,) = run(
        forward_body,
        "forward",
        [((4, 64, 1024), BF16)],
        VM,
        [
            VM((2304, 1024), F32),
            VM((512, 1024), BF16),
            VM((256, 128), F32),
            pltpu.SemaphoreType.DMA((2,)),
        ],
        18,
        20 * PRODUCT,
        place,
        whole,
        kernel,
        demod,
        far=(1, 3),
    )
    pieces = run(
        quarter_body, "quarter_sum", [((4, 80, 128), BF16)] * 4, VM, [VM((16, 2304), F32)],
        6, 10**7, place, *quarters,
    )
    total = pieces[0].astype(F32)
    for k in (1, 2, 3):
        total = total + moved_by(pieces[k], "x", k).astype(F32)
    pieces = total.astype(BF16)
    pieces, out = lax.optimization_barrier((pieces, out))
    outs = [out[0]] + [moved_by(out[k], "x", k) for k in (1, 2, 3)]
    parts = [pieces[0]] + [moved_by(pieces[k], "l", k) for k in (1, 2, 3)]
    output, input_grad, style_grad = run(
        finish_body,
        "finish",
        [((4, 64, 1024), BF16), ((4, 64, 1024), BF16), ((4, 64), F32)],
        (HB, VM, VM),
        [pltpu.SemaphoreType.DMA((4,))],
        8,
        10**7,
        place,
        *outs,
        back_parts,
        images,
        scale,
    )
    input_grad, style_grad, *parts = lax.optimization_barrier((input_grad, style_grad, *parts))
    total = sum((part.astype(F32) for part in parts[1:]), parts[0].astype(F32))
    total = (total * (1.0 / 128)).reshape(5, 16, 2, 64)
    weight_grad = total.transpose(0, 2, 3, 1).reshape(10, 64, 16)[:9]
    return (output, input_grad, style_grad, weight_grad)


def solution(mesh):
    return jax.shard_map(
        on_device,
        mesh=mesh,
        in_specs=(
            P("dp", "cout", None),
            P("dp", None),
            P(None, "cout", "dp"),
            P("dp", "cout", None),
        ),
        out_specs=(
            P("dp", "cout", None),
            P("dp", "cout", None),
            P("dp", "cout"),
            P(None, "cout", "dp"),
        ),
        check_vma=False,
    )
```

```python
import jax
import jax.numpy as jnp
from jax import lax
from jax.experimental import pallas as pl
from jax.experimental.pallas import tpu as pltpu
from jax.sharding import PartitionSpec as P

RES = 32
epsilon = 1e-08
tap_steps = [(-1, -1), (-1, 0), (-1, 1), (0, -1), (0, 0), (0, 1), (1, -1), (1, 0), (1, 1)]
F32 = jnp.float32
BF16 = jnp.bfloat16
HIGH = lax.Precision.HIGHEST
BOTH = ("dp", "cout")
SIZES = {"l": 4, "y": 4, "c": 2, "h": 2, "x": 4}
MIB = 1 << 20


def flat_index(at):
    return ((at["l"] * 4 + at["y"]) * 2 + at["c"]) * 8 + at["h"] * 4 + at["x"]


def places(names):
    if not names:
        return [{}]
    return [{**rest, names[0]: v} for v in range(SIZES[names[0]]) for rest in places(names[1:])]


def exchange(blocks, along):
    others = [name for name in "lychx" if name not in along]
    groups = [[flat_index({**fixed, **at}) for at in places(along)] for fixed in places(others)]
    return lax.all_to_all(blocks, BOTH, 0, 0, axis_index_groups=groups, tiled=True)


def moved_by(value, name, step):
    pairs = []
    for at in places("lychx"):
        to = {**at, name: (at[name] + step) % SIZES[name]}
        pairs.append((flat_index(at), flat_index(to)))
    return lax.ppermute(value, BOTH, pairs)


def inside(row_step, col_step):
    pixel = lax.broadcasted_iota(jnp.int32, (1, RES * RES), 1)
    row = pixel // RES + row_step
    col = pixel % RES + col_step
    return (row >= 0) & (row < RES) & (col >= 0) & (col < RES)


def shifted(value, row_step, col_step):
    offset = row_step * RES + col_step
    if offset == 0:
        return value
    rolled = pltpu.roll(value, (-offset) % (RES * RES), 1)
    return jnp.where(inside(row_step, col_step), rolled, 0.0)


def rows_of(place, k, l):
    return (((place[0] + l) % 4) * 4 + (place[1] + k) % 4) * 32


def ready_body(place, whole, out):
    del whole
    for index in range(4):
        out[index] = place[index]


def gradient_body(
    place, style, cot0, cot1, cot2, cot3, whole, own0, own1, own2, own3, other0, other1, other2, other3,
    demod_out, send_out, keep_out, back_out, kernel_out,
    moved, grad, images, kernel_t, scaled_t, energy_t, inner, demod, send, keep, back, sems,
):
    core = place[2]
    sources = []
    for k, (own, other) in enumerate(
        ((own0, other0), (own1, other1), (own2, other2), (own3, other3))
    ):
        sources += [(k, own, core), (k, other, 1 - core)]

    def copy(index, source, target):
        return pltpu.make_async_copy(source, target, sems.at[index])

    copy(4, whole, images).start()
    for k, source in enumerate((cot0, cot1, cot2, cot3)):
        block = ((place[3] + 4 - k) % 4) * 64

        @pl.loop(0, 2)
        def _(half):
            value = source[pl.ds(pl.multiple_of(half * 32, 32), 32), :].astype(F32)
            for t, (a, c) in enumerate(tap_steps):
                row = pl.multiple_of(t * 256 + block + half * 32, 32)
                moved[pl.ds(row, 32), :] = shifted(value, -a, -c).astype(BF16)

    for k, source, at_core in sources:

        @pl.loop(0, 4)
        def _(l):
            row = pl.multiple_of(rows_of(place, k, l) + at_core * 16, 16)
            piece = source[l]
            kernel_t[pl.ds(row, 16), :] = piece
            wide = piece.astype(F32)
            total = jnp.zeros((16, 256), F32)
            for t in range(9):
                part = wide[:, t * 256 : (t + 1) * 256]
                total = total + part * part
            energy_t[pl.ds(row, 16), :] = total

    row_style = style[...]
    style_col = jnp.transpose(jnp.broadcast_to(row_style[:1], (128, 512)))
    square = style_col * style_col
    energy = jnp.concatenate(
        [
            jnp.sum(energy_t[:, j * 128 : (j + 1) * 128] * square, axis=0, keepdims=True)
            for j in range(2)
        ],
        axis=1,
    )
    factor = lax.rsqrt(energy + epsilon)
    demod[...] = jnp.transpose(jnp.broadcast_to(factor, (128, 256)))
    copy(0, demod, demod_out).start()
    copy(6, kernel_t, kernel_out).start()

    copy(4, whole, images).wait()

    @pl.loop(0, 9)
    def _(t):
        lanes = pl.ds(pl.multiple_of(t * 256, 256), 256)
        grad[:, lanes] = lax.dot_general(
            images[...], moved[lanes, :], (((1,), (1,)), ((), ())), preferred_element_type=F32
        )

    inner[...] = jnp.zeros((16, 256), F32)

    @pl.loop(0, 32)
    def _(step):
        row = pl.multiple_of(step * 16, 16)
        dots = jnp.zeros((16, 256), F32)
        for t in range(9):
            lanes = slice(t * 256, (t + 1) * 256)
            part = kernel_t[pl.ds(row, 16), lanes].astype(F32)
            dots = dots + part * grad[pl.ds(row, 16), lanes]
            scaled_t[pl.ds(row, 16), lanes] = (part * factor).astype(BF16)
        inner[...] += dots

    norm = jnp.sum(inner[...], axis=0, keepdims=True)
    slope = -0.5 * norm * (factor * factor * factor)
    style_sum = jnp.sum(energy_t[...] * slope[:1], axis=1, keepdims=True)
    back[:, 1024:1152] = (2.0 * style_col * style_sum).astype(BF16)
    for j in range(2):
        lanes = slice(j * 128, (j + 1) * 128)
        energy_t[:, lanes] = 2.0 * square * slope[:1, lanes]

    side = slice(1024, 1152)
    copy(3, back.at[:, side], back_out.at[:, side]).start()

    def back_copy(step):
        lanes = pl.ds(pl.multiple_of(step * 256, 256), 256)
        return copy(7 + step, back.at[:, lanes], back_out.at[:, lanes])

    def terms_copy(step):
        return copy(11 + step, send.at[step], send_out.at[step])

    def keep_copy(step):
        return copy(15 + step, keep.at[step], keep_out.at[step])

    @pl.loop(0, 4)
    def _(step):
        lanes = pl.ds(pl.multiple_of(step * 256, 256), 256)
        back[:, lanes] = jnp.dot(
            scaled_t[...], moved[:, lanes], preferred_element_type=F32
        ).astype(BF16)
        for l in range(4):
            for target, at_core in ((keep, core), (send, 1 - core)):
                row = pl.multiple_of(rows_of(place, step, l) + at_core * 16, 16)
                radial = energy_t[pl.ds(row, 16), :]
                for t in range(9):
                    taps = slice(t * 256, (t + 1) * 256)
                    part = kernel_t[pl.ds(row, 16), taps].astype(F32)
                    term = grad[pl.ds(row, 16), taps] * factor + part * radial
                    target[step, l, :, taps] = term.astype(target.dtype)
        back_copy(step).start()
        terms_copy(step).start()
        keep_copy(step).start()

    copy(0, demod, demod_out).wait()
    copy(3, back.at[:, side], back_out.at[:, side]).wait()
    copy(6, kernel_t, kernel_out).wait()

    @pl.loop(0, 4)
    def _(step):
        back_copy(step).wait()
        terms_copy(step).wait()
        keep_copy(step).wait()


def forward_body(place, whole, kernel_in, demod_in, out, products, kernel_t, images, demod, sems):
    copies = [
        pltpu.make_async_copy(source, target, sems.at[index])
        for index, (source, target) in enumerate(
            ((kernel_in, kernel_t), (whole, images), (demod_in, demod))
        )
    ]
    for copy in copies:
        copy.start()
    for copy in copies:
        copy.wait()

    @pl.loop(0, 4)
    def _(step):
        lanes = pl.ds(pl.multiple_of(step * 256, 256), 256)
        products[:, lanes] = lax.dot_general(
            kernel_t[...], images[:, lanes], (((0,), (0,)), ((), ())), preferred_element_type=F32
        )

    @pl.loop(0, 8)
    def _(step):
        k, half = step // 2, step % 2
        row = pl.multiple_of(((place[3] + k) % 4) * 64 + half * 32, 32)
        total = products[pl.ds(4 * 256 + row, 32), :]
        for t, (a, c) in enumerate(tap_steps):
            if t != 4:
                total = total + shifted(products[pl.ds(t * 256 + row, 32), :], a, c)
        factor = demod[pl.ds(row, 32), :]
        for j in range(8):
            lanes = slice(j * 128, (j + 1) * 128)
            place_at = pl.ds(pl.multiple_of(half * 32, 32), 32)
            out[k, place_at, lanes] = (factor * total[:, lanes]).astype(BF16)


def pair_body(keep, received, *outs):
    for k, out in enumerate(outs):

        @pl.loop(0, 4)
        def _(l):
            out[l] = (keep[k, l] + received[k, l].astype(F32)).astype(BF16)


def quarter_body(place, part0, part1, part2, part3, out0, out1, out2, out3, sums):
    low = lax.broadcasted_iota(jnp.int32, (16, 128), 1) < 64

    @pl.loop(0, 4)
    def _(l):
        total = part0[l].astype(F32)
        for part in (part1, part2, part3):
            total = total + part[l].astype(F32)
        sums[...] = total
        for k, out in enumerate((out0, out1, out2, out3)):
            column = (place[3] + k) % 4
            even = column % 2 == 0

            def block(t):
                start = pl.multiple_of(t * 256 + (column // 2) * 128, 128)
                value = sums[:, pl.ds(start, 128)]
                return value, pltpu.roll(value, 64, 1)

            for pair in range(5):
                first, first_rolled = block(2 * pair)
                left = jnp.where(even, first, first_rolled)
                right = jnp.zeros((16, 128), F32)
                if pair < 4:
                    second, second_rolled = block(2 * pair + 1)
                    right = jnp.where(even, second_rolled, second)
                packed = jnp.where(low, left, right).astype(BF16)
                out[l, pair * 16 : (pair + 1) * 16, :] = packed


def finish_body(
    place, part0, part1, part2, part3, back, images, scale, out, input_grad, style_grad, sems
):
    copies = []
    for k, part in enumerate((part0, part1, part2, part3)):
        slot = (place[3] + 4 - k) % 4
        copies.append(pltpu.make_async_copy(part, out.at[slot], sems.at[k]))
    for copy in copies:
        copy.start()
    lane = lax.broadcasted_iota(jnp.int32, (64, 128), 1)
    columns = jnp.zeros((64, 128), F32)
    for b in range(4):
        total = jnp.zeros((64, 128), F32)
        for j in range(8):
            lanes = slice(j * 128, (j + 1) * 128)
            value = back[0, b, :, lanes].astype(F32) + back[1, b, :, lanes].astype(F32)
            input_grad[b, :, lanes] = (value * scale[b]).astype(BF16)
            total = total + value * images[b, :, lanes].astype(F32)
        side = slice(1024, 1152)
        side = back[0, b, :, side].astype(F32) + back[1, b, :, side].astype(F32)
        column = jnp.sum(total, axis=1, keepdims=True) + side[:, :1]
        columns = jnp.where(lane == b, column, columns)
    style_grad[...] = jnp.transpose(columns)[:4]
    for copy in copies:
        copy.wait()


PRODUCT = 2 * 512 * 2304 * 1024
VM = pltpu.VMEM
HB = pltpu.HBM


def run(body, name, outs, out_space, scratch, mib, flops, *args, far=()):
    def space(index, arg):
        if arg.dtype == jnp.int32:
            return pltpu.SMEM
        return HB if index in far else VM

    return pl.pallas_call(
        body,
        out_shape=tuple(jax.ShapeDtypeStruct(*one) for one in outs),
        in_specs=[pl.BlockSpec(memory_space=space(*one)) for one in enumerate(args)],
        out_specs=tuple(
            pl.BlockSpec(memory_space=out_space[n] if isinstance(out_space, tuple) else out_space)
            for n in range(len(outs))
        ),
        scratch_shapes=scratch,
        compiler_params=pltpu.CompilerParams(vmem_limit_bytes=mib * MIB),
        cost_estimate=pl.CostEstimate(flops=flops, bytes_accessed=MIB, transcendentals=256),
        name=name,
    )(*args)


def ring_take(parts, start):
    return lax.dynamic_slice_in_dim(jnp.concatenate([parts, parts]), start, 4, 0)


def on_device(images, styles, weight, cotangent):
    seat = lax.axis_index("cout")
    spot = lax.axis_index("dp")
    column = seat % 4
    place = jnp.stack([spot // 8, (spot // 2) % 4, spot % 2, column]).astype(jnp.int32)
    local_styles = lax.dynamic_slice_in_dim(styles, seat * 64, 64, 1)
    style = jnp.broadcast_to(lax.dynamic_slice_in_dim(styles, column, 1, 0), (8, 512))

    packed = jnp.transpose(weight, (2, 0, 1)).reshape(9, 1024)
    stages = [packed] + [moved_by(packed, "l", -k) for k in (1, 2, 3)]
    rows = jnp.pad(jnp.concatenate(stages), ((0, 4), (0, 0)))
    scale = jnp.broadcast_to(local_styles[:, :, None], (4, 64, 128))
    modulated = (images.astype(F32) * local_styles[:, :, None]).astype(BF16)
    rows, twice = lax.optimization_barrier((rows, jnp.concatenate([modulated, modulated])))
    whole = exchange(twice, "hx").reshape(512, 1024)

    sides = [rows] + [moved_by(rows, "x", k) for k in (1, 2, 3)]
    taps = jnp.stack([sides[k][:36] for k in (0, 3, 2, 1)])
    taps = ring_take(taps, (4 - column) % 4)
    near = taps.reshape(4, 4, 16, 9, 64).transpose(1, 2, 3, 0, 4).reshape(4, 16, 2304)
    turned = [lax.dynamic_index_in_dim(cotangent, (column + k) % 4, 0, False) for k in range(4)]
    near, *turned = lax.optimization_barrier((near, *turned))
    cots = [turned[0]] + [moved_by(turned[k], "x", k) for k in (1, 2, 3)]
    own = [near] + [moved_by(near, "y", -k) for k in (1, 2, 3)]
    kernels = own + [moved_by(one, "c", 1) for one in own]

    (ready,) = run(
        ready_body, "ready", [((4,), jnp.int32)], pltpu.SMEM, [], 1, 12 * PRODUCT, place, whole,
        far=(1,),
    )
    blocks = (4, 4, 16, 2304)
    demod, send, keep, back, kernel_t = run(
        gradient_body,
        "gradient",
        [
            ((256, 128), F32),
            (blocks, BF16),
            (blocks, F32),
            ((512, 1152), BF16),
            ((512, 2304), BF16),
        ],
        HB,
        [
            VM((2304, 1024), BF16),
            VM((512, 2304), F32),
            VM((512, 1024), BF16),
            VM((512, 2304), BF16),
            VM((512, 2304), BF16),
            VM((512, 256), F32),
            VM((16, 256), F32),
            VM((256, 128), F32),
            VM(blocks, BF16),
            VM(blocks, F32),
            VM((512, 1152), BF16),
            pltpu.SemaphoreType.DMA((19,)),
        ],
        32,
        2 * PRODUCT,
        ready,
        style,
        *cots,
        whole,
        *kernels,
        far=(6,),
    )
    received = moved_by(send, "c", 1)
    (out,) = run(
        forward_body,
        "forward",
        [((4, 64, 1024), BF16)],
        VM,
        [
            VM((2304, 1024), F32),
            VM((512, 2304), BF16),
            VM((512, 1024), BF16),
            VM((256, 128), F32),
            pltpu.SemaphoreType.DMA((3,)),
        ],
        54,
        20 * PRODUCT,
        place,
        whole,
        kernel_t,
        demod,
        far=(1, 2, 3),
    )
    halves = run(
        pair_body, "pair_sum", [((4, 16, 2304), BF16)] * 4, VM, [], 8, 10**7, keep, received
    )
    halves, back = lax.optimization_barrier((halves, back))
    back_parts = exchange(back.reshape(8, 64, 1152), "hx").reshape(2, 4, 64, 1152)
    quarters = [halves[0]] + [moved_by(halves[k], "y", k) for k in (1, 2, 3)]
    pieces = run(
        quarter_body, "quarter_sum", [((4, 80, 128), BF16)] * 4, VM, [VM((16, 2304), F32)],
        6, 10**7, place, *quarters,
    )
    total = pieces[0].astype(F32)
    for k in (1, 2, 3):
        total = total + moved_by(pieces[k], "x", k).astype(F32)
    pieces = total.astype(BF16)
    pieces, out = lax.optimization_barrier((pieces, out))
    outs = [out[0]] + [moved_by(out[k], "x", k) for k in (1, 2, 3)]
    parts = [pieces[0]] + [moved_by(pieces[k], "l", k) for k in (1, 2, 3)]
    output, input_grad, style_grad = run(
        finish_body,
        "finish",
        [((4, 64, 1024), BF16), ((4, 64, 1024), BF16), ((4, 64), F32)],
        (HB, VM, VM),
        [pltpu.SemaphoreType.DMA((4,))],
        8,
        10**7,
        place,
        *outs,
        back_parts,
        images,
        scale,
    )
    input_grad, style_grad, *parts = lax.optimization_barrier((input_grad, style_grad, *parts))
    total = sum((part.astype(F32) for part in parts[1:]), parts[0].astype(F32))
    total = (total * (1.0 / 128)).reshape(5, 16, 2, 64)
    weight_grad = total.transpose(0, 2, 3, 1).reshape(10, 64, 16)[:9]
    return (output, input_grad, style_grad, weight_grad)


def solution(mesh):
    return jax.shard_map(
        on_device,
        mesh=mesh,
        in_specs=(
            P("dp", "cout", None),
            P("dp", None),
            P(None, "cout", "dp"),
            P("dp", "cout", None),
        ),
        out_specs=(
            P("dp", "cout", None),
            P("dp", "cout", None),
            P("dp", "cout"),
            P(None, "cout", "dp"),
        ),
        check_vma=False,
    )
```
